512 devices in a mesh: dp: 8 (over z_hi, y), shard: 64 (over x, z_lo, core).
Axes of the slice: x: 4, y: 4, z: 16 (z_hi: 2, z_lo: 8; z = z_hi * 8 + z_lo), core: 2. Of those that a mesh axis runs over, the one named last changes fastest.
Arguments:
- grad_out: bfloat16 [8, 16, 128, 8, 256], P('dp', None, 'shard'), may hold values from -6 to 6
- saved_mid: bfloat16 [8, 16, 64, 4, 512], P('dp', None, 'shard'), may hold values from -6 to 6
- norm_gain: float32 [512], replicated, may hold values from 0.25 to 1.75
- high_kernel: bfloat16 [512, 27, 256], P('shard'), may hold values from -0.078125 to 0.078125
- low_kernel: bfloat16 [256, 27, 512], P('shard'), may hold values from -0.0546875 to 0.0546875
Outputs:
- grad_in: bfloat16 [8, 64, 64, 1, 256], P('dp', 'shard')
- gain_grad: float32 [512], replicated
The draws below stay inside these ranges and needn't reach their ends.
All inputs are finite; a program needn't handle non-finite values.
Results may differ from the reference program's by a relative error of at most 0.0049.
Values may be sent and summed in bfloat16 or wider, within the bound.
No kernel may reach another device: no remote copies, remote signals or barrier semaphores. Data moves between devices by JAX's collectives and lax.ppermute only.
A program may use at most 64 MiB of HBM per device.

```python
import math
import jax
import jax.numpy as jnp
from jax import lax

C_LOW = 256
C_MID = 512
C_HIGH = 256
FRAMES = 16
COL_LOW = 4
COL_SPLIT = 4
CLIPS = 8
ROWS_LOW = 64
ROWS_HIGH = 128
COL_HIGH = 8
POSITIONS = 131072


def shard_levels(own_key, extent, pieces, least, largest):
    gain, own = 1.0, jax.random.fold_in(own_key, 6)
    for axis_at, shards_of in pieces:
        steps = jnp.exp(jax.random.uniform(jax.random.fold_in(own, axis_at), (shards_of,), jnp.float32, least / len(pieces), largest / len(pieces)))
        gain = gain * jnp.repeat(steps, extent[axis_at] // shards_of).reshape([-1 if axis == axis_at else 1 for axis in range(len(extent))])
    return gain


def scatter_about(key, extent, deviation, most, split=(), kind=jnp.bfloat16):
    gain = shard_levels(key, extent, split, -0.22, 0.18) if split else 1.0
    array = jax.random.normal(key, extent, jnp.float32) * deviation * gain
    return jnp.minimum(jnp.maximum(array, -most), most).astype(kind)


def setup_inputs(seed: int = 0) -> dict:
    seeds = jax.random.split(jax.random.key(seed), 6)
    return {
        "grad_out": scatter_about(seeds[0], (CLIPS, FRAMES, ROWS_HIGH, COL_HIGH, C_HIGH), 1.0, 6.0, ((0, 8), (2, 64))),
        "saved_mid": scatter_about(seeds[1], (CLIPS, FRAMES, ROWS_LOW, COL_LOW, C_MID), 1.0, 6.0, ((0, 8), (2, 64))),
        "norm_gain": jnp.clip(1.0 + 0.15 * jax.random.normal(seeds[2], (C_MID,), jnp.float32), 0.25, 1.75),
        "high_kernel": scatter_about(seeds[3], (C_MID, 27, C_HIGH), (27 * C_HIGH) ** -0.5, 0.078125, ((0, 64),)),
        "low_kernel": scatter_about(seeds[4], (C_LOW, 27, C_MID), (27 * C_MID) ** -0.5, 0.0546875, ((0, 64),)),
    }


EPSILON = 1e-06

def back_conv(grad, kernel):
    count = kernel.shape[0]
    outer = kernel.shape[2]
    taps = kernel.astype(jnp.float32).reshape(count, 3, 3, 3, outer)[:, ::-1, ::-1, ::-1, :]
    taps = jnp.transpose(taps, (1, 2, 3, 4, 0))
    result = lax.conv_general_dilated(grad.astype(jnp.float32)[None], taps, (1, 1, 1), ((0, 2), (1, 1), (1, 1)), dimension_numbers=('NDHWC', 'DHWIO', 'NDHWC'), precision=lax.Precision.HIGHEST)
    return result[0]

def reference(grad_out, saved_mid, norm_gain, high_kernel, low_kernel):

    def norm_back(pair):
        grad_clip, mid_clip = pair
        norm_grad = back_conv(grad_clip, high_kernel)
        frames, rows_high, cols_high, channels = norm_grad.shape
        blocks = norm_grad.reshape(frames, rows_high // 2, 2, cols_high // 2, 2, channels)
        mid_values = mid_clip.astype(jnp.float32)[:, :, None, :, None, :]
        inverse_rms = lax.rsqrt(lax.optimization_barrier(jnp.mean(mid_values * mid_values, axis=-1, keepdims=True)) + EPSILON)
        scaled = mid_values * inverse_rms
        normed = scaled * norm_gain
        gate_sig = jax.nn.sigmoid(normed)
        normed_grad = blocks * gate_sig * (1.0 + normed * (1.0 - gate_sig))
        local_gain = lax.optimization_barrier(jnp.sum(normed_grad * scaled, axis=(0, 1, 2, 3, 4)))
        gained = normed_grad * norm_gain
        pre_grad = inverse_rms * (gained - scaled * lax.optimization_barrier(jnp.mean(gained * scaled, axis=-1, keepdims=True)))
        mid_grad = lax.optimization_barrier(jnp.sum(pre_grad, axis=(2, 4))).astype(jnp.bfloat16)
        return (mid_grad, local_gain)
    mid_grads, gains = lax.map(norm_back, (grad_out, saved_mid))
    gain_grad = lax.optimization_barrier(jnp.sum(gains, axis=0)) / math.sqrt(POSITIONS)
    whole = lax.map(lambda clip: back_conv(clip, low_kernel).astype(jnp.bfloat16), mid_grads)
    clips, frames, rows_low, cols_low, inputs = whole.shape
    col_dev = cols_low // COL_SPLIT
    arranged = whole.reshape(clips, frames, rows_low, COL_SPLIT, col_dev, inputs)
    arranged = jnp.transpose(arranged, (0, 1, 3, 2, 4, 5))
    grad_in = arranged.reshape(clips, frames * COL_SPLIT, rows_low, col_dev, inputs)
    return (grad_in, gain_grad)
```

```python
import math

import jax
import jax.numpy as jnp
from jax import lax
from jax.experimental import pallas as pl
from jax.experimental.pallas import tpu as pltpu
from jax.sharding import Mesh
from jax.sharding import PartitionSpec as P

EPSILON = 1e-06
F32 = jnp.float32
BF16 = jnp.bfloat16
NEAR = (0, 1, -1, 2)
FAR = (4, -3, 3, -2)
OFFSETS = tuple(o for pair in zip(NEAR, FAR) for o in pair)
NT = (((1,), (1,)), ((), ()))


def iota(shape, dim):
    return lax.broadcasted_iota(jnp.int32, shape, dim)


def owner_z(slot, z):
    offset = jnp.zeros_like(slot)
    for n, o in enumerate(OFFSETS):
        offset = jnp.where(slot == n, o % 8, offset)
    return (z + offset) & 7


def row_shift(value, by):
    rows = value.shape[0]
    by = by % rows
    return value if by == 0 else pltpu.roll(value, rows - by, 0)


def half_turn(value):
    return pltpu.roll(value, 64, 1)


def full_mid(parts_ref, source):
    return jnp.concatenate(
        [parts_ref[source, 384:448, :], parts_ref[source, 448:512, :]], axis=1
    )


def inverse_rms(mid):
    return lax.rsqrt(jnp.mean(mid * mid, axis=1, keepdims=True) + EPSILON)


def high_kernel_body(place_ref, parts_ref, weight_ref, gain_ref, out_ref, gain_out_ref, taps_ref, wide_ref):
    x, c, z = place_ref[0], place_ref[1], place_ref[2]
    for dy in range(3):
        for dw in range(3):
            for dt in range(3):
                tap = 9 * (2 - dt) + 3 * (2 - dy) + dw
                for j in range(4):
                    at = (dw * 4 + dt) * 64 + 16 * j
                    taps_ref[dy, at : at + 16, :] = weight_ref[j, tap]
            at = (dw * 4 + 3) * 64
            taps_ref[dy, at : at + 64, :] = jnp.zeros((64, 256), BF16)
    row = iota((256, 256), 0)
    column_high = row & 7
    frame = (iota((256, 128), 0) >> 3) & 15
    low_half = iota((128, 128), 1) < 64
    for pair in range(4):
        rows = jnp.concatenate(
            [parts_ref[2 * pair, 0:384, :], parts_ref[2 * pair + 1, 0:384, :]], axis=0
        )
        product = sum(
            lax.dot_general(
                rows[128 * dy : 128 * dy + 512], taps_ref[dy], NT, preferred_element_type=F32
            )
            for dy in range(3)
        )
        pooled = jnp.concatenate(
            [product[0:128] + product[128:256], product[256:384] + product[384:512]], axis=0
        )
        after = jnp.where(column_high < 7, row_shift(pooled[:, 0:256], 1), 0.0)
        before = jnp.where(column_high > 0, row_shift(pooled[:, 512:768], -1), 0.0)
        moved = after + pooled[:, 256:512] + before
        moved = moved + row_shift(moved, 1)
        now, later = moved[:, 0:128], moved[:, 128:256]
        total = now
        total = total + jnp.where(frame < 15, row_shift(half_turn(now), 8), 0.0)
        total = total + jnp.where(frame < 14, row_shift(later, 16), 0.0)
        wide_ref[128 * pair : 128 * pair + 128, :] = jnp.where(
            low_half, total[0:128], half_turn(total[128:256])
        )
    summed = jnp.concatenate(
        [wide_ref[pl.ds(128 * pair, 64, stride=2), :] for pair in range(4)], axis=0
    )
    lane = iota((1, 128), 1)
    slot = (lane >> 3) & 7
    target = 128 * x + 16 * owner_z(slot, z) + 8 * c + (lane & 7)
    channel = iota((512, 128), 0)
    hit = channel == target
    half = iota((512, 128), 1) >> 6
    picks = [jnp.where(hit & (half == y), 1.0, 0.0).astype(BF16) for y in range(2)]
    mids = [
        jnp.concatenate([full_mid(parts_ref, 2 * pair + y) for pair in range(4)], axis=0)
        for y in range(2)
    ]
    mid = sum(
        jnp.dot(m, s, preferred_element_type=F32) for m, s in zip(mids, picks)
    )
    rms = [inverse_rms(m.astype(F32)) for m in mids]
    scaled = mid * jnp.where(iota((256, 128), 1) < 64, rms[0], rms[1])
    gain = jnp.dot(
        jnp.broadcast_to(gain_ref[...], (8, 512)),
        jnp.where(hit, 1.0, 0.0),
        precision=lax.Precision.HIGHEST,
        preferred_element_type=F32,
    )[0:1]
    normed = scaled * gain
    gate = jax.nn.sigmoid(normed)
    grad = summed * (gate * (1.0 + normed * (1.0 - gate)))
    out_ref[...] = (grad * gain).astype(BF16)
    terms = jnp.sum(grad * scaled, axis=0, keepdims=True)
    terms = terms + half_turn(terms)
    source = iota((128, 128), 0)
    place = (source & 64) + 8 * owner_z((source >> 3) & 7, z) + (source & 7)
    order = jnp.where(place == iota((128, 128), 1), 1.0, 0.0)
    gain_out_ref[...] = jnp.dot(
        jnp.broadcast_to(terms, (8, 128)),
        order,
        precision=lax.Precision.HIGHEST,
        preferred_element_type=F32,
    )


def low_kernel_body(place_ref, grads_ref, parts_ref, weight_ref, out_ref, turned_ref):
    z = place_ref[2]
    source = iota((256, 256), 0)
    target = (
        ((source >> 6) & 1) * 128
        + owner_z((source >> 3) & 7, z) * 16
        + (source >> 7) * 8
        + (source & 7)
    )
    order = jnp.where(target == iota((256, 256), 1), 1.0, 0.0).astype(BF16)
    placed = [
        jnp.dot(
            jnp.concatenate([grads_ref[2 * x], grads_ref[2 * x + 1]], axis=1),
            order,
            preferred_element_type=F32,
        )
        for x in range(4)
    ]
    halves = []
    for y in range(2):
        grad = jnp.concatenate([p[:, 128 * y : 128 * y + 128] for p in placed], axis=1)
        mid = jnp.concatenate(
            [full_mid(parts_ref, 2 * pair + y) for pair in range(4)], axis=0
        ).astype(F32)
        rms = inverse_rms(mid)
        scaled = mid * rms
        mean = jnp.mean(grad * scaled, axis=1, keepdims=True)
        halves.append((rms * (grad - scaled * mean)).astype(BF16))
    grads = jnp.concatenate(halves, axis=0)
    row = iota((512, 128), 0)
    frame = (row >> 2) & 15
    column = row & 3
    total = jnp.zeros((512, 128), F32)
    for a in range(3):
        for c in range(3):
            at = 16 * (3 * a + c)
            taps = jnp.concatenate([weight_ref[n, at : at + 16, :] for n in range(8)], axis=0)
            product = lax.dot_general(grads, taps, NT, preferred_element_type=F32)
            moved = row_shift(product, 4 * (2 - a) + 1 - c)
            keep = (frame + 2 - a < 16) & (column + 1 - c >= 0) & (column + 1 - c < 4)
            total = total + jnp.where(keep, moved, 0.0)
    result = total[0:256] + pltpu.roll(total[256:512], 4, 1)
    for pair in range(4):
        turned_ref[:, pair, :] = result[64 * pair : 64 * pair + 64]
    turned_ref[:, 4:8, :] = jnp.zeros((64, 4, 128), F32)
    out_ref[...] = turned_ref[...].astype(BF16)


def join_body(scale, parts_ref, out_ref, gain_ref):
    parts = parts_ref[...].astype(F32)
    strips = [
        jnp.concatenate([parts[16 * x + 2 * z + c] for z in range(8)], axis=0)
        for x in range(4)
        for c in range(2)
    ]
    wide = jnp.concatenate([s.astype(BF16) for s in strips], axis=1)
    lane = iota((64, 1024), 1)
    row_out = iota((64, 64), 0)
    row_in = iota((64, 64), 1)
    pair, z = row_in & 7, row_in >> 3
    joined = jnp.zeros((64, 1024), F32)
    for n in range(4):
        pick = (row_out == 16 * pair + 2 * z - 1 + n) & (pair < 4)
        placed = jnp.dot(
            jnp.where(pick, 1.0, 0.0).astype(BF16), wide, preferred_element_type=F32
        )
        joined = jnp.where(((lane >> 2) & 3) == n, placed, joined)
    source = iota((1024, 256), 0)
    target = (
        (source >> 8) * 64 + ((source >> 4) & 7) * 8 + ((source >> 7) & 1) * 4 + (source & 3)
    )
    order = jnp.where(target == iota((1024, 256), 1), 1.0, 0.0).astype(BF16)
    out_ref[...] = jnp.dot(
        joined.astype(BF16), order, preferred_element_type=F32
    ).astype(BF16)
    low_half = iota((1, 128), 1) < 64
    lines = []
    for x in range(4):
        pieces = []
        for c in range(2):
            piece = sum(parts[16 * x + 2 * z + c, 4:5, :] for z in range(8))
            pieces.append(piece + half_turn(piece))
        lines.append(jnp.where(low_half, pieces[0], pieces[1]))
    lines = jnp.concatenate(lines + lines, axis=0)
    source = iota((128, 128), 0)
    target = ((source >> 3) & 7) * 16 + (source >> 6) * 8 + (source & 7)
    order = jnp.where(target == iota((128, 128), 1), 1.0, 0.0)
    gain_ref[...] = (
        jnp.dot(lines, order, precision=lax.Precision.HIGHEST, preferred_element_type=F32)[0:4]
        * scale
    )


def whole():
    return pl.BlockSpec(memory_space=pltpu.VMEM)


def scalars():
    return pl.BlockSpec(memory_space=pltpu.SMEM)


PARAMS = pltpu.CompilerParams(vmem_limit_bytes=40 * 1024 * 1024)


def ring_pairs(distances):
    pairs = []
    for zh in range(2):
        for y in range(4):
            for zl in range(8):
                for c in range(2):
                    by = distances[y]
                    if by == 4 and c == 1:
                        by = -4
                    at = (zh * 8 + zl + by) % 16
                    source = ((at // 8 * 4 + y) * 8 + at % 8) * 2 + c
                    pairs.append((source, ((zh * 4 + y) * 8 + zl) * 2 + c))
    return pairs


def shards(grad_out, saved_mid, norm_gain, high_kernel, low_kernel):
    x, z, c = (lax.axis_index(n) for n in ("x", "zl", "c"))
    place = jnp.stack([x, c, z]).astype(jnp.int32)
    ring = ("zh", "y", "zl", "c")
    group = ("x", "c")
    shard = ("x", "zl", "c")

    low = jnp.transpose(low_kernel.reshape(4, 3, 3, 3, 512), (1, 3, 2, 0, 4))
    low = jnp.pad(low, ((0, 0), (0, 0), (0, 1), (0, 0), (0, 0))).reshape(144, 512)
    low_all = lax.all_gather(low, "zl", axis=0)

    grad = grad_out[0]
    edge = jnp.where(c == 0, grad[:, 0], grad[:, 1])
    halo_pairs = [(s, s - 1) for s in range(2, 64, 2)] + [(s, s + 1) for s in range(1, 62, 2)]
    halo = lax.ppermute(edge, shard, halo_pairs)

    high = jnp.transpose(high_kernel, (1, 0, 2))
    near = lax.ppermute(high, ring, ring_pairs(NEAR))
    far = lax.ppermute(high, ring, ring_pairs(FAR))

    own = jnp.transpose(grad, (1, 0, 2, 3)).reshape(256, 256)
    halo = halo.reshape(128, 256)
    rows = jnp.where(
        c == 0,
        jnp.concatenate([halo, own], axis=0),
        jnp.concatenate([own, halo], axis=0),
    )
    mid = saved_mid.reshape(64, 512)
    chunk = jnp.concatenate([rows, mid[:, 0:256], mid[:, 256:512]], axis=0)
    parts = lax.all_to_all(
        jnp.broadcast_to(chunk[None], (8, 512, 256)), group, split_axis=0, concat_axis=0, tiled=True
    )
    high_all = lax.all_gather(jnp.concatenate([near, far], axis=1), "y", axis=0)

    grads, gain_terms = pl.pallas_call(
        high_kernel_body,
        out_shape=(
            jax.ShapeDtypeStruct((256, 128), BF16),
            jax.ShapeDtypeStruct((8, 128), F32),
        ),
        in_specs=[scalars(), whole(), whole(), whole()],
        out_specs=(whole(), whole()),
        scratch_shapes=[pltpu.VMEM((3, 768, 256), BF16), pltpu.VMEM((512, 128), F32)],
        compiler_params=PARAMS,
        name="high_conv",
    )(place, parts, high_all, norm_gain.reshape(1, 512))

    gathered = lax.all_gather(grads, group, axis=0)
    for axis, pairs in (
        ("y", [(i, i ^ 1) for i in range(4)]),
        ("y", [(i, i ^ 2) for i in range(4)]),
        ("zh", [(0, 1), (1, 0)]),
    ):
        gain_terms = gain_terms + lax.ppermute(gain_terms, axis, pairs)

    partial = pl.pallas_call(
        low_kernel_body,
        out_shape=jax.ShapeDtypeStruct((64, 8, 128), BF16),
        in_specs=[scalars(), whole(), whole(), whole()],
        out_specs=whole(),
        scratch_shapes=[pltpu.VMEM((64, 8, 128), F32)],
        compiler_params=PARAMS,
        name="low_conv",
    )(place, gathered, parts, low_all)

    head = lax.reduce_precision(gain_terms, 8, 7)
    tail = gain_terms - head
    line = jnp.where(lax.broadcasted_iota(jnp.int32, (8, 128), 1) < 64, head, tail).astype(BF16)
    is_gain = lax.broadcasted_iota(jnp.int32, (64, 8, 128), 1) == 4
    outgoing = jnp.where(is_gain, line[None], partial)
    incoming = lax.all_to_all(outgoing, shard, split_axis=0, concat_axis=0, tiled=True)

    positions = 8 * 16 * 128 * 8
    grad_in, gain_grad = pl.pallas_call(
        lambda *refs: join_body(1.0 / math.sqrt(positions), *refs),
        out_shape=(
            jax.ShapeDtypeStruct((64, 256), BF16),
            jax.ShapeDtypeStruct((4, 128), F32),
        ),
        in_specs=[whole()],
        out_specs=(whole(), whole()),
        compiler_params=PARAMS,
        name="join",
    )(incoming)
    return (grad_in.reshape(1, 1, 64, 1, 256), gain_grad.reshape(512))


def solution(mesh):
    fine = Mesh(mesh.devices.reshape(2, 4, 4, 8, 2), ("zh", "y", "x", "zl", "c"))
    dp, shard = ("zh", "y"), ("x", "zl", "c")
    return jax.shard_map(
        shards,
        mesh=fine,
        in_specs=(
            P(dp, None, shard, None, None),
            P(dp, None, shard, None, None),
            P(),
            P(shard, None, None),
            P(shard, None, None),
        ),
        out_specs=(P(dp, shard, None, None, None), P()),
        check_vma=False,
    )
```

```python
import math

import jax
import jax.numpy as jnp
from jax import lax
from jax.experimental import pallas as pl
from jax.experimental.pallas import tpu as pltpu
from jax.sharding import Mesh
from jax.sharding import PartitionSpec as P

EPSILON = 1e-06
F32 = jnp.float32
BF16 = jnp.bfloat16
NEAR = ((0, 1, -1, 2), (0, -1, 1, 2))
FAR = ((4, -3, 3, -2), (-4, 3, -3, -2))
NT = (((1,), (1,)), ((), ()))


def iota(shape, dim):
    return lax.broadcasted_iota(jnp.int32, shape, dim)


def owner_z(slot, z, c):
    offset = jnp.zeros_like(slot)
    for y in range(4):
        for n, table in enumerate((NEAR, FAR)):
            by = jnp.where(c == 0, table[0][y] % 8, table[1][y] % 8)
            offset = jnp.where(slot == 2 * y + n, by, offset)
    return (z + offset) & 7


def slot_of(owner, z, c):
    distance = (owner - z) & 7
    slot = jnp.int32(0)
    for y in range(4):
        for n, table in enumerate((NEAR, FAR)):
            by = jnp.where(c == 0, table[0][y] % 8, table[1][y] % 8)
            slot = jnp.where(distance == by, 2 * y + n, slot)
    return slot


def row_shift(value, by):
    rows = value.shape[0]
    by = by % rows
    return value if by == 0 else pltpu.roll(value, rows - by, 0)


def half_turn(value):
    return pltpu.roll(value, 64, 1)


def full_mid(parts_ref, source):
    return jnp.concatenate(
        [parts_ref[source, 384:448, :], parts_ref[source, 448:512, :]], axis=1
    )


def inverse_rms(mid):
    return lax.rsqrt(jnp.mean(mid * mid, axis=1, keepdims=True) + EPSILON)


def pack_body(place_ref, rows_ref, halo_ref, mid_ref, out_ref):
    c = place_ref[1]
    for core in range(2):

        @pl.when(c == core)
        def _():
            for n in range(8):
                if core == 0:
                    block = (halo_ref[...], rows_ref[:, 0], rows_ref[:, 1])
                else:
                    block = (rows_ref[:, 0], rows_ref[:, 1], halo_ref[...])
                for r in range(3):
                    out_ref[n, r] = block[r]

    for n in range(8):
        out_ref[n, 3] = mid_ref[...]


def high_kernel_body(place_ref, parts_ref, weight_ref, gain_ref, out_ref, gain_out_ref, taps_ref, wide_ref):
    x, c, z = place_ref[0], place_ref[1], place_ref[2]
    for dy in range(3):
        for dw in range(3):
            for dt in range(3):
                tap = 9 * (2 - dt) + 3 * (2 - dy) + dw
                for j in range(4):
                    at = (dw * 4 + dt) * 64 + 16 * j
                    taps_ref[dy, at : at + 16, :] = weight_ref[j, 16 * tap : 16 * tap + 16, :]
            at = (dw * 4 + 3) * 64
            taps_ref[dy, at : at + 64, :] = jnp.zeros((64, 256), BF16)
    row = iota((256, 256), 0)
    column_high = row & 7
    frame = (iota((256, 128), 0) >> 3) & 15
    low_half = iota((128, 128), 1) < 64
    for pair in range(4):
        rows = jnp.concatenate(
            [parts_ref[2 * pair, 0:384, :], parts_ref[2 * pair + 1, 0:384, :]], axis=0
        )
        product = sum(
            lax.dot_general(
                rows[128 * dy : 128 * dy + 512], taps_ref[dy], NT, preferred_element_type=F32
            )
            for dy in range(3)
        )
        pooled = jnp.concatenate(
            [product[0:128] + product[128:256], product[256:384] + product[384:512]], axis=0
        )
        after = jnp.where(column_high < 7, row_shift(pooled[:, 0:256], 1), 0.0)
        before = jnp.where(column_high > 0, row_shift(pooled[:, 512:768], -1), 0.0)
        moved = after + pooled[:, 256:512] + before
        moved = moved + row_shift(moved, 1)
        now, later = moved[:, 0:128], moved[:, 128:256]
        total = now
        total = total + jnp.where(frame < 15, row_shift(half_turn(now), 8), 0.0)
        total = total + jnp.where(frame < 14, row_shift(later, 16), 0.0)
        wide_ref[128 * pair : 128 * pair + 128, :] = jnp.where(
            low_half, total[0:128], half_turn(total[128:256])
        )
    summed = jnp.concatenate(
        [wide_ref[pl.ds(128 * pair, 64, stride=2), :] for pair in range(4)], axis=0
    )
    lane = iota((1, 128), 1)
    slot = (lane >> 3) & 7
    target = 128 * x + 16 * owner_z(slot, z, c) + 8 * c + (lane & 7)
    channel = iota((512, 128), 0)
    hit = channel == target
    half = iota((512, 128), 1) >> 6
    picks = [jnp.where(hit & (half == y), 1.0, 0.0).astype(BF16) for y in range(2)]
    mids = [
        jnp.concatenate([full_mid(parts_ref, 2 * pair + y) for pair in range(4)], axis=0)
        for y in range(2)
    ]
    mid = sum(
        jnp.dot(m, s, preferred_element_type=F32) for m, s in zip(mids, picks)
    )
    rms = [inverse_rms(m.astype(F32)) for m in mids]
    scaled = mid * jnp.where(iota((256, 128), 1) < 64, rms[0], rms[1])
    gain = jnp.dot(
        jnp.broadcast_to(gain_ref[...], (8, 512)),
        jnp.where(hit, 1.0, 0.0),
        precision=lax.Precision.HIGHEST,
        preferred_element_type=F32,
    )[0:1]
    normed = scaled * gain
    gate = jax.nn.sigmoid(normed)
    grad = summed * (gate * (1.0 + normed * (1.0 - gate)))
    sent = (grad * gain).astype(BF16)
    out_ref[...] = sent
    terms = jnp.sum(grad * scaled, axis=0, keepdims=True)
    terms = terms + half_turn(terms)
    source = iota((128, 128), 0)
    place = (source & 64) + 8 * owner_z((source >> 3) & 7, z, c) + (source & 7)
    order = jnp.where(place == iota((128, 128), 1), 1.0, 0.0)
    terms = jnp.dot(
        jnp.broadcast_to(terms, (8, 128)),
        order,
        precision=lax.Precision.HIGHEST,
        preferred_element_type=F32,
    )
    gain_out_ref[...] = terms


def low_kernel_body(place_ref, grads_ref, parts_ref, weight_ref, out_ref, turned_ref):
    c, z = place_ref[1], place_ref[2]
    source = iota((256, 256), 0)
    target = (
        ((source >> 6) & 1) * 128
        + owner_z((source >> 3) & 7, z, source >> 7) * 16
        + (source >> 7) * 8
        + (source & 7)
    )
    order = jnp.where(target == iota((256, 256), 1), 1.0, 0.0).astype(BF16)
    placed = [
        jnp.dot(
            jnp.concatenate([grads_ref[2 * x], grads_ref[2 * x + 1]], axis=1),
            order,
            preferred_element_type=F32,
        )
        for x in range(4)
    ]
    halves = []
    for y in range(2):
        grad = jnp.concatenate([p[:, 128 * y : 128 * y + 128] for p in placed], axis=1)
        mid = jnp.concatenate(
            [full_mid(parts_ref, 2 * pair + y) for pair in range(4)], axis=0
        ).astype(F32)
        rms = inverse_rms(mid)
        scaled = mid * rms
        mean = jnp.mean(grad * scaled, axis=1, keepdims=True)
        halves.append((rms * (grad - scaled * mean)).astype(BF16))
    grads = jnp.concatenate(halves, axis=0)
    row = iota((512, 128), 0)
    frame = (row >> 2) & 15
    column = row & 3
    total = jnp.zeros((512, 128), F32)
    slots = [slot_of(n, z, c) for n in range(8)]
    for a in range(3):
        for b in range(3):
            at = 16 * (3 * a + b)
            taps = jnp.concatenate(
                [
                    jnp.concatenate(
                        [weight_ref[n, at : at + 16, :], weight_ref[n, 144 + at : 160 + at, :]],
                        axis=1,
                    )
                    for n in slots
                ],
                axis=0,
            )
            product = lax.dot_general(grads, taps, NT, preferred_element_type=F32)
            moved = row_shift(product, 4 * (2 - a) + 1 - b)
            keep = (frame + 2 - a < 16) & (column + 1 - b >= 0) & (column + 1 - b < 4)
            total = total + jnp.where(keep, moved, 0.0)
    result = total[0:256] + pltpu.roll(total[256:512], 4, 1)
    for pair in range(4):
        turned_ref[:, pair, :] = result[64 * pair : 64 * pair + 64]
    out_ref[...] = turned_ref[...].astype(BF16)


def close_body(rows_ref, terms_ref, out_ref):
    terms = terms_ref[0]
    for n in range(1, 4):
        terms = terms + terms_ref[n]
    head = terms.astype(BF16).astype(F32)
    line = jnp.where(iota((8, 128), 1) < 64, head, terms - head)[0:2].astype(BF16)
    out_ref[:, 0] = rows_ref[:, 0:2]
    out_ref[:, 1] = rows_ref[:, 2:4]
    out_ref[:, 2] = jnp.broadcast_to(line[None], (64, 2, 128))


def join_body(scale, parts_ref, out_ref, gain_ref, rows_ref):
    for n in range(3):
        rows_ref[:, 2 * n : 2 * n + 2, :] = parts_ref[:, n].astype(F32)
    rows_ref[:, 6:8, :] = jnp.zeros((64, 2, 128), F32)
    parts = rows_ref[...]
    strips = [
        jnp.concatenate([parts[16 * x + 2 * z + c] for z in range(8)], axis=0)
        for x in range(4)
        for c in range(2)
    ]
    wide = jnp.concatenate([s.astype(BF16) for s in strips], axis=1)
    lane = iota((64, 1024), 1)
    row_out = iota((64, 64), 0)
    row_in = iota((64, 64), 1)
    pair, z = row_in & 7, row_in >> 3
    joined = jnp.zeros((64, 1024), F32)
    for n in range(4):
        pick = (row_out == 16 * pair + 2 * z - 1 + n) & (pair < 4)
        placed = jnp.dot(
            jnp.where(pick, 1.0, 0.0).astype(BF16), wide, preferred_element_type=F32
        )
        joined = jnp.where(((lane >> 2) & 3) == n, placed, joined)
    source = iota((1024, 256), 0)
    target = (
        (source >> 8) * 64 + ((source >> 4) & 7) * 8 + ((source >> 7) & 1) * 4 + (source & 3)
    )
    order = jnp.where(target == iota((1024, 256), 1), 1.0, 0.0).astype(BF16)
    out_ref[...] = jnp.dot(
        joined.astype(BF16), order, preferred_element_type=F32
    ).astype(BF16)
    low_half = iota((1, 128), 1) < 64
    lines = []
    for x in range(4):
        pieces = []
        for c in range(2):
            piece = sum(parts[16 * x + 2 * z + c, 4:5, :] for z in range(8))
            pieces.append(piece + half_turn(piece))
        lines.append(jnp.where(low_half, pieces[0], pieces[1]))
    lines = jnp.concatenate(lines + lines, axis=0)
    source = iota((128, 128), 0)
    target = ((source >> 3) & 7) * 16 + (source >> 6) * 8 + (source & 7)
    order = jnp.where(target == iota((128, 128), 1), 1.0, 0.0)
    gain_ref[...] = (
        jnp.dot(lines, order, precision=lax.Precision.HIGHEST, preferred_element_type=F32)[0:4]
        * scale
    )


def whole():
    return pl.BlockSpec(memory_space=pltpu.VMEM)


def scalars():
    return pl.BlockSpec(memory_space=pltpu.SMEM)


PARAMS = pltpu.CompilerParams(vmem_limit_bytes=40 * 1024 * 1024)


def ring_pairs(distances):
    pairs = []
    for zh in range(2):
        for y in range(4):
            for zl in range(8):
                for c in range(2):
                    at = (zh * 8 + zl + distances[c][y]) % 16
                    source = ((at // 8 * 4 + y) * 8 + at % 8) * 2 + c
                    pairs.append((source, ((zh * 4 + y) * 8 + zl) * 2 + c))
    return pairs


def shards(grad_out, saved_mid, norm_gain, high_kernel, low_kernel):
    x, z, c = (lax.axis_index(n) for n in ("x", "zl", "c"))
    place = jnp.stack([x, c, z]).astype(jnp.int32)
    ring = ("zh", "y", "zl", "c")
    group = ("x", "c")
    shard = ("x", "zl", "c")

    grad = grad_out[0]
    edge = jnp.where(c == 0, grad[:, 0], grad[:, 1])
    halo_pairs = [(s, s - 1) for s in range(2, 64, 2)] + [(s, s + 1) for s in range(1, 62, 2)]
    halo = lax.ppermute(edge, shard, halo_pairs)

    high = jnp.transpose(high_kernel, (1, 0, 2)).reshape(216, 256)
    low = jnp.transpose(low_kernel.reshape(4, 3, 3, 3, 2, 256), (4, 1, 3, 2, 0, 5))
    low = jnp.pad(low, ((0, 0), (0, 0), (0, 0), (0, 1), (0, 0), (0, 0))).reshape(288, 256)
    kernels = jnp.concatenate([high, low], axis=0)
    near = lax.ppermute(kernels, ring, ring_pairs(NEAR))
    far = lax.ppermute(kernels, ring, ring_pairs(FAR))

    mid = saved_mid.reshape(64, 512)
    mid = jnp.concatenate([mid[:, 0:256], mid[:, 256:512]], axis=0).reshape(16, 8, 256)
    packed = pl.pallas_call(
        pack_body,
        out_shape=jax.ShapeDtypeStruct((8, 4, 16, 8, 256), BF16),
        in_specs=[scalars()] + [whole()] * 3,
        out_specs=whole(),
        compiler_params=PARAMS,
        name="pack_rows",
    )(place, grad, halo, mid)
    parts = lax.all_to_all(packed.reshape(8, 512, 256), group, split_axis=0, concat_axis=0, tiled=True)
    high = jnp.concatenate([near[:216].reshape(27, 8, 256), far[:216].reshape(27, 8, 256)], axis=1)
    high_all = lax.all_gather(high.reshape(432, 256), "y", axis=0)
    low = jnp.stack([near[216:], far[216:]], axis=0)
    low_all = lax.all_gather(low, "y", axis=0, tiled=True)

    grads, gain_terms = pl.pallas_call(
        high_kernel_body,
        out_shape=(
            jax.ShapeDtypeStruct((256, 128), BF16),
            jax.ShapeDtypeStruct((8, 128), F32),
        ),
        in_specs=[scalars(), whole(), whole(), whole()],
        out_specs=(whole(), whole()),
        scratch_shapes=[pltpu.VMEM((3, 768, 256), BF16), pltpu.VMEM((512, 128), F32)],
        compiler_params=PARAMS,
        name="high_conv",
    )(place, parts, high_all, norm_gain.reshape(1, 512))

    halves = [(z, (z + 4) % 16 if z % 8 >= 4 else (z - 4) % 16) for z in range(16)]
    other = lax.ppermute(gain_terms, ("zh", "zl"), halves)
    gathered = lax.all_gather(grads, group, axis=0)
    other, gathered = lax.optimization_barrier((other, gathered))
    clips = lax.all_to_all(
        jnp.broadcast_to((gain_terms + other)[None], (4, 8, 128)), "y", split_axis=0, concat_axis=0, tiled=True
    )

    partial = pl.pallas_call(
        low_kernel_body,
        out_shape=jax.ShapeDtypeStruct((64, 4, 128), BF16),
        in_specs=[scalars(), whole(), whole(), whole()],
        out_specs=whole(),
        scratch_shapes=[pltpu.VMEM((64, 4, 128), F32)],
        compiler_params=PARAMS,
        name="low_conv",
    )(place, gathered, parts, low_all)

    outgoing = pl.pallas_call(
        close_body,
        out_shape=jax.ShapeDtypeStruct((64, 3, 2, 128), BF16),
        in_specs=[whole(), whole()],
        out_specs=whole(),
        compiler_params=PARAMS,
        name="close",
    )(partial, clips)
    outgoing = outgoing.reshape(192, 2, 128)
    incoming = lax.all_to_all(outgoing, shard, split_axis=0, concat_axis=0, tiled=True)

    positions = 8 * 16 * 128 * 8
    grad_in, gain_grad = pl.pallas_call(
        lambda *refs: join_body(1.0 / math.sqrt(positions), *refs),
        out_shape=(
            jax.ShapeDtypeStruct((64, 256), BF16),
            jax.ShapeDtypeStruct((4, 128), F32),
        ),
        in_specs=[whole()],
        out_specs=(whole(), whole()),
        scratch_shapes=[pltpu.VMEM((64, 8, 128), F32)],
        compiler_params=PARAMS,
        name="join",
    )(incoming.reshape(64, 3, 2, 128))
    return (grad_in.reshape(1, 1, 64, 1, 256), gain_grad.reshape(512))


def solution(mesh):
    fine = Mesh(mesh.devices.reshape(2, 4, 4, 8, 2), ("zh", "y", "x", "zl", "c"))
    dp, shard = ("zh", "y"), ("x", "zl", "c")
    return jax.shard_map(
        shards,
        mesh=fine,
        in_specs=(
            P(dp, None, shard, None, None),
            P(dp, None, shard, None, None),
            P(),
            P(shard, None, None),
            P(shard, None, None),
        ),
        out_specs=(P(dp, shard, None, None, None), P()),
        check_vma=False,
    )
```

```python
import math

import jax
import jax.numpy as jnp
from jax import lax
from jax.experimental import pallas as pl
from jax.experimental.pallas import tpu as pltpu
from jax.sharding import Mesh
from jax.sharding import PartitionSpec as P

EPSILON = 1e-06
F32 = jnp.float32
BF16 = jnp.bfloat16
NEAR = ((0, 1, -1, 2), (0, -1, 1, 2))
FAR = ((4, -3, 3, -2), (-4, 3, -3, -2))
NT = (((1,), (1,)), ((), ()))


def iota(shape, dim):
    return lax.broadcasted_iota(jnp.int32, shape, dim)


def owner_z(slot, z, c):
    offset = jnp.zeros_like(slot)
    for y in range(4):
        for n, table in enumerate((NEAR, FAR)):
            by = jnp.where(c == 0, table[0][y] % 8, table[1][y] % 8)
            offset = jnp.where(slot == 2 * y + n, by, offset)
    return (z + offset) & 7


def slot_of(owner, z, c):
    distance = (owner - z) & 7
    slot = jnp.int32(0)
    for y in range(4):
        for n, table in enumerate((NEAR, FAR)):
            by = jnp.where(c == 0, table[0][y] % 8, table[1][y] % 8)
            slot = jnp.where(distance == by, 2 * y + n, slot)
    return slot


def row_shift(value, by):
    rows = value.shape[0]
    by = by % rows
    return value if by == 0 else pltpu.roll(value, rows - by, 0)


def half_turn(value):
    return pltpu.roll(value, 64, 1)


def full_mid(edges_ref, source):
    return jnp.concatenate(
        [edges_ref[source, 128:192, :], edges_ref[source, 192:256, :]], axis=1
    )


def inverse_rms(mid):
    return lax.rsqrt(jnp.mean(mid * mid, axis=1, keepdims=True) + EPSILON)


def high_kernel_body(place_ref, parts_ref, edges_ref, weight_ref, gain_ref, out_ref, gain_out_ref, taps_ref, wide_ref):
    x, c, z = place_ref[0], place_ref[1], place_ref[2]
    for dy in range(3):
        for dw in range(3):
            for dt in range(3):
                tap = 9 * (2 - dt) + 3 * (2 - dy) + dw
                for j in range(4):
                    at = (dw * 4 + dt) * 64 + 16 * j
                    taps_ref[dy, at : at + 16, :] = weight_ref[j, 16 * tap : 16 * tap + 16, :]
            at = (dw * 4 + 3) * 64
            taps_ref[dy, at : at + 64, :] = jnp.zeros((64, 256), BF16)
    row = iota((256, 256), 0)
    column_high = row & 7
    frame = (iota((256, 128), 0) >> 3) & 15
    low_half = iota((128, 128), 1) < 64
    for pair in range(4):
        rows = jnp.concatenate(
            [
                edges_ref[2 * pair, 0:128, :],
                parts_ref[2 * pair],
                parts_ref[2 * pair + 1],
                edges_ref[2 * pair + 1, 0:128, :],
            ],
            axis=0,
        )
        product = sum(
            lax.dot_general(
                rows[128 * dy : 128 * dy + 512], taps_ref[dy], NT, preferred_element_type=F32
            )
            for dy in range(3)
        )
        pooled = jnp.concatenate(
            [product[0:128] + product[128:256], product[256:384] + product[384:512]], axis=0
        )
        after = jnp.where(column_high < 7, row_shift(pooled[:, 0:256], 1), 0.0)
        before = jnp.where(column_high > 0, row_shift(pooled[:, 512:768], -1), 0.0)
        moved = after + pooled[:, 256:512] + before
        moved = moved + row_shift(moved, 1)
        now, later = moved[:, 0:128], moved[:, 128:256]
        total = now
        total = total + jnp.where(frame < 15, row_shift(half_turn(now), 8), 0.0)
        total = total + jnp.where(frame < 14, row_shift(later, 16), 0.0)
        wide_ref[128 * pair : 128 * pair + 128, :] = jnp.where(
            low_half, total[0:128], half_turn(total[128:256])
        )
    summed = jnp.concatenate(
        [wide_ref[pl.ds(128 * pair, 64, stride=2), :] for pair in range(4)], axis=0
    )
    lane = iota((1, 128), 1)
    slot = (lane >> 3) & 7
    target = 128 * x + 16 * owner_z(slot, z, c) + 8 * c + (lane & 7)
    channel = iota((512, 128), 0)
    hit = channel == target
    half = iota((512, 128), 1) >> 6
    picks = [jnp.where(hit & (half == y), 1.0, 0.0).astype(BF16) for y in range(2)]
    mids = [
        jnp.concatenate([full_mid(edges_ref, 2 * pair + y) for pair in range(4)], axis=0)
        for y in range(2)
    ]
    mid = sum(
        jnp.dot(m, s, preferred_element_type=F32) for m, s in zip(mids, picks)
    )
    rms = [inverse_rms(m.astype(F32)) for m in mids]
    scaled = mid * jnp.where(iota((256, 128), 1) < 64, rms[0], rms[1])
    gain = jnp.dot(
        jnp.broadcast_to(gain_ref[...], (8, 512)),
        jnp.where(hit, 1.0, 0.0),
        precision=lax.Precision.HIGHEST,
        preferred_element_type=F32,
    )[0:1]
    normed = scaled * gain
    gate = jax.nn.sigmoid(normed)
    grad = summed * (gate * (1.0 + normed * (1.0 - gate)))
    sent = (grad * gain).astype(BF16)
    out_ref[...] = sent
    terms = jnp.sum(grad * scaled, axis=0, keepdims=True)
    terms = terms + half_turn(terms)
    source = iota((128, 128), 0)
    place = (source & 64) + 8 * owner_z((source >> 3) & 7, z, c) + (source & 7)
    order = jnp.where(place == iota((128, 128), 1), 1.0, 0.0)
    terms = jnp.dot(
        jnp.broadcast_to(terms, (8, 128)),
        order,
        precision=lax.Precision.HIGHEST,
        preferred_element_type=F32,
    )
    gain_out_ref[...] = terms


def low_kernel_body(place_ref, grads_ref, edges_ref, weight_ref, out_ref, turned_ref):
    c, z = place_ref[1], place_ref[2]
    source = iota((256, 256), 0)
    target = (
        ((source >> 6) & 1) * 128
        + owner_z((source >> 3) & 7, z, source >> 7) * 16
        + (source >> 7) * 8
        + (source & 7)
    )
    order = jnp.where(target == iota((256, 256), 1), 1.0, 0.0).astype(BF16)
    placed = [
        jnp.dot(
            jnp.concatenate([grads_ref[2 * x], grads_ref[2 * x + 1]], axis=1),
            order,
            preferred_element_type=F32,
        )
        for x in range(4)
    ]
    halves = []
    for y in range(2):
        grad = jnp.concatenate([p[:, 128 * y : 128 * y + 128] for p in placed], axis=1)
        mid = jnp.concatenate(
            [full_mid(edges_ref, 2 * pair + y) for pair in range(4)], axis=0
        ).astype(F32)
        rms = inverse_rms(mid)
        scaled = mid * rms
        mean = jnp.mean(grad * scaled, axis=1, keepdims=True)
        halves.append((rms * (grad - scaled * mean)).astype(BF16))
    grads = jnp.concatenate(halves, axis=0)
    row = iota((512, 128), 0)
    frame = (row >> 2) & 15
    column = row & 3
    total = jnp.zeros((512, 128), F32)
    slots = [slot_of(n, z, c) for n in range(8)]
    for a in range(3):
        for b in range(3):
            at = 16 * (3 * a + b)
            taps = jnp.concatenate(
                [
                    jnp.concatenate(
                        [weight_ref[n, at : at + 16, :], weight_ref[n, 144 + at : 160 + at, :]],
                        axis=1,
                    )
                    for n in slots
                ],
                axis=0,
            )
            product = lax.dot_general(grads, taps, NT, preferred_element_type=F32)
            moved = row_shift(product, 4 * (2 - a) + 1 - b)
            keep = (frame + 2 - a < 16) & (column + 1 - b >= 0) & (column + 1 - b < 4)
            total = total + jnp.where(keep, moved, 0.0)
    result = total[0:256] + pltpu.roll(total[256:512], 4, 1)
    for pair in range(4):
        turned_ref[:, pair, :] = result[64 * pair : 64 * pair + 64]
    out_ref[...] = turned_ref[...].astype(BF16)


def close_body(rows_ref, terms_ref, out_ref):
    terms = terms_ref[0]
    for n in range(1, 4):
        terms = terms + terms_ref[n]
    head = terms.astype(BF16).astype(F32)
    line = jnp.where(iota((8, 128), 1) < 64, head, terms - head)[0:2].astype(BF16)
    out_ref[:, 0] = rows_ref[:, 0:2]
    out_ref[:, 1] = rows_ref[:, 2:4]
    out_ref[:, 2] = jnp.broadcast_to(line[None], (64, 2, 128))


def join_body(scale, parts_ref, out_ref, gain_ref, rows_ref):
    for n in range(3):
        rows_ref[:, 2 * n : 2 * n + 2, :] = parts_ref[:, n].astype(F32)
    rows_ref[:, 6:8, :] = jnp.zeros((64, 2, 128), F32)
    parts = rows_ref[...]
    strips = [
        jnp.concatenate([parts[16 * x + 2 * z + c] for z in range(8)], axis=0)
        for x in range(4)
        for c in range(2)
    ]
    wide = jnp.concatenate([s.astype(BF16) for s in strips], axis=1)
    lane = iota((64, 1024), 1)
    row_out = iota((64, 64), 0)
    row_in = iota((64, 64), 1)
    pair, z = row_in & 7, row_in >> 3
    joined = jnp.zeros((64, 1024), F32)
    for n in range(4):
        pick = (row_out == 16 * pair + 2 * z - 1 + n) & (pair < 4)
        placed = jnp.dot(
            jnp.where(pick, 1.0, 0.0).astype(BF16), wide, preferred_element_type=F32
        )
        joined = jnp.where(((lane >> 2) & 3) == n, placed, joined)
    source = iota((1024, 256), 0)
    target = (
        (source >> 8) * 64 + ((source >> 4) & 7) * 8 + ((source >> 7) & 1) * 4 + (source & 3)
    )
    order = jnp.where(target == iota((1024, 256), 1), 1.0, 0.0).astype(BF16)
    out_ref[...] = jnp.dot(
        joined.astype(BF16), order, preferred_element_type=F32
    ).astype(BF16)
    low_half = iota((1, 128), 1) < 64
    lines = []
    for x in range(4):
        pieces = []
        for c in range(2):
            piece = sum(parts[16 * x + 2 * z + c, 4:5, :] for z in range(8))
            pieces.append(piece + half_turn(piece))
        lines.append(jnp.where(low_half, pieces[0], pieces[1]))
    lines = jnp.concatenate(lines + lines, axis=0)
    source = iota((128, 128), 0)
    target = ((source >> 3) & 7) * 16 + (source >> 6) * 8 + (source & 7)
    order = jnp.where(target == iota((128, 128), 1), 1.0, 0.0)
    gain_ref[...] = (
        jnp.dot(lines, order, precision=lax.Precision.HIGHEST, preferred_element_type=F32)[0:4]
        * scale
    )


def whole():
    return pl.BlockSpec(memory_space=pltpu.VMEM)


def scalars():
    return pl.BlockSpec(memory_space=pltpu.SMEM)


PARAMS = pltpu.CompilerParams(vmem_limit_bytes=40 * 1024 * 1024)


def ring_pairs(distances):
    pairs = []
    for zh in range(2):
        for y in range(4):
            for zl in range(8):
                for c in range(2):
                    at = (zh * 8 + zl + distances[c][y]) % 16
                    source = ((at // 8 * 4 + y) * 8 + at % 8) * 2 + c
                    pairs.append((source, ((zh * 4 + y) * 8 + zl) * 2 + c))
    return pairs


def shards(grad_out, saved_mid, norm_gain, high_kernel, low_kernel):
    x, z, c = (lax.axis_index(n) for n in ("x", "zl", "c"))
    place = jnp.stack([x, c, z]).astype(jnp.int32)
    ring = ("zh", "y", "zl", "c")
    group = ("x", "c")
    shard = ("x", "zl", "c")

    grad = grad_out[0]
    edge = jnp.where(c == 0, grad[:, 0], grad[:, 1])
    halo_pairs = [(s, s - 1) for s in range(2, 64, 2)] + [(s, s + 1) for s in range(1, 62, 2)]
    halo = lax.ppermute(edge, shard, halo_pairs)

    high = jnp.transpose(high_kernel, (1, 0, 2)).reshape(216, 256)
    low = jnp.transpose(low_kernel.reshape(4, 3, 3, 3, 2, 256), (4, 1, 3, 2, 0, 5))
    low = jnp.pad(low, ((0, 0), (0, 0), (0, 0), (0, 1), (0, 0), (0, 0))).reshape(288, 256)
    kernels = jnp.concatenate([high, low], axis=0)
    near = lax.ppermute(kernels, ring, ring_pairs(NEAR))
    far = lax.ppermute(kernels, ring, ring_pairs(FAR))

    def spread(block):
        return lax.all_to_all(
            jnp.broadcast_to(block[None], (8, 256, 256)), group, split_axis=0, concat_axis=0, tiled=True
        )

    parts = spread(jnp.transpose(grad, (1, 0, 2, 3)).reshape(256, 256))
    mid = saved_mid.reshape(64, 512)
    near, far, parts, halo = lax.optimization_barrier((near, far, parts, halo))
    edges = spread(jnp.concatenate([halo.reshape(128, 256), mid[:, 0:256], mid[:, 256:512]], axis=0))
    high = jnp.concatenate([near[:216].reshape(27, 8, 256), far[:216].reshape(27, 8, 256)], axis=1)
    high_all = lax.all_gather(high.reshape(432, 256), "y", axis=0)
    low = jnp.stack([near[216:], far[216:]], axis=0)
    low_all = lax.all_gather(low, "y", axis=0, tiled=True)

    grads, gain_terms = pl.pallas_call(
        high_kernel_body,
        out_shape=(
            jax.ShapeDtypeStruct((256, 128), BF16),
            jax.ShapeDtypeStruct((8, 128), F32),
        ),
        in_specs=[scalars()] + [whole()] * 4,
        out_specs=(whole(), whole()),
        scratch_shapes=[pltpu.VMEM((3, 768, 256), BF16), pltpu.VMEM((512, 128), F32)],
        compiler_params=PARAMS,
        name="high_conv",
    )(place, parts, edges, high_all, norm_gain.reshape(1, 512))

    halves = [(z, (z + 4) % 16 if z % 8 >= 4 else (z - 4) % 16) for z in range(16)]
    other = lax.ppermute(gain_terms, ("zh", "zl"), halves)
    gathered = lax.all_gather(grads, group, axis=0)
    other, gathered = lax.optimization_barrier((other, gathered))
    clips = lax.all_to_all(
        jnp.broadcast_to((gain_terms + other)[None], (4, 8, 128)), "y", split_axis=0, concat_axis=0, tiled=True
    )

    partial = pl.pallas_call(
        low_kernel_body,
        out_shape=jax.ShapeDtypeStruct((64, 4, 128), BF16),
        in_specs=[scalars(), whole(), whole(), whole()],
        out_specs=whole(),
        scratch_shapes=[pltpu.VMEM((64, 4, 128), F32)],
        compiler_params=PARAMS,
        name="low_conv",
    )(place, gathered, edges, low_all)

    outgoing = pl.pallas_call(
        close_body,
        out_shape=jax.ShapeDtypeStruct((64, 3, 2, 128), BF16),
        in_specs=[whole(), whole()],
        out_specs=whole(),
        compiler_params=PARAMS,
        name="close",
    )(partial, clips)
    outgoing = outgoing.reshape(192, 2, 128)
    incoming = lax.all_to_all(outgoing, shard, split_axis=0, concat_axis=0, tiled=True)

    positions = 8 * 16 * 128 * 8
    grad_in, gain_grad = pl.pallas_call(
        lambda *refs: join_body(1.0 / math.sqrt(positions), *refs),
        out_shape=(
            jax.ShapeDtypeStruct((64, 256), BF16),
            jax.ShapeDtypeStruct((4, 128), F32),
        ),
        in_specs=[whole()],
        out_specs=(whole(), whole()),
        scratch_shapes=[pltpu.VMEM((64, 8, 128), F32)],
        compiler_params=PARAMS,
        name="join",
    )(incoming.reshape(64, 3, 2, 128))
    return (grad_in.reshape(1, 1, 64, 1, 256), gain_grad.reshape(512))


def solution(mesh):
    fine = Mesh(mesh.devices.reshape(2, 4, 4, 8, 2), ("zh", "y", "x", "zl", "c"))
    dp, shard = ("zh", "y"), ("x", "zl", "c")
    return jax.shard_map(
        shards,
        mesh=fine,
        in_specs=(
            P(dp, None, shard, None, None),
            P(dp, None, shard, None, None),
            P(),
            P(shard, None, None),
            P(shard, None, None),
        ),
        out_specs=(P(dp, shard, None, None, None), P()),
        check_vma=False,
    )
```

```python
import math

import jax
import jax.numpy as jnp
from jax import lax
from jax.experimental import pallas as pl
from jax.experimental.pallas import tpu as pltpu
from jax.sharding import Mesh
from jax.sharding import PartitionSpec as P

EPSILON = 1e-06
F32 = jnp.float32
BF16 = jnp.bfloat16
NEAR = ((0, 1, -1, 2), (0, -1, 1, 2))
FAR = ((4, -3, 3, -2), (-4, 3, -3, -2))
NT = (((1,), (1,)), ((), ()))


def iota(shape, dim):
    return lax.broadcasted_iota(jnp.int32, shape, dim)


def owner_z(slot, z, c):
    offset = jnp.zeros_like(slot)
    for y in range(4):
        for n, table in enumerate((NEAR, FAR)):
            by = jnp.where(c == 0, table[0][y] % 8, table[1][y] % 8)
            offset = jnp.where(slot == 2 * y + n, by, offset)
    return (z + offset) & 7


def slot_of(owner, z, c):
    distance = (owner - z) & 7
    slot = jnp.int32(0)
    for y in range(4):
        for n, table in enumerate((NEAR, FAR)):
            by = jnp.where(c == 0, table[0][y] % 8, table[1][y] % 8)
            slot = jnp.where(distance == by, 2 * y + n, slot)
    return slot


def row_shift(value, by):
    rows = value.shape[0]
    by = by % rows
    return value if by == 0 else pltpu.roll(value, rows - by, 0)


def half_turn(value):
    return pltpu.roll(value, 64, 1)


def full_mid(edges_ref, source):
    return jnp.concatenate(
        [edges_ref[source, 128:192, :], edges_ref[source, 192:256, :]], axis=1
    )


def inverse_rms(mid):
    return lax.rsqrt(jnp.mean(mid * mid, axis=1, keepdims=True) + EPSILON)


def high_kernel_body(place_ref, parts_ref, edges_ref, weight_ref, gain_ref, out_ref, gain_out_ref, taps_ref, wide_ref):
    x, c, z = place_ref[0], place_ref[1], place_ref[2]
    for dy in range(3):
        for dw in range(3):
            for dt in range(3):
                tap = 9 * (2 - dt) + 3 * (2 - dy) + dw
                for j in range(4):
                    at = (dw * 4 + dt) * 64 + 16 * j
                    taps_ref[dy, at : at + 16, :] = weight_ref[j, 16 * tap : 16 * tap + 16, :]
            at = (dw * 4 + 3) * 64
            taps_ref[dy, at : at + 64, :] = jnp.zeros((64, 256), BF16)
    row = iota((256, 256), 0)
    column_high = row & 7
    frame = (iota((256, 128), 0) >> 3) & 15
    low_half = iota((128, 128), 1) < 64
    for pair in range(4):
        rows = jnp.concatenate(
            [
                edges_ref[2 * pair, 0:128, :],
                parts_ref[2 * pair],
                parts_ref[2 * pair + 1],
                edges_ref[2 * pair + 1, 0:128, :],
            ],
            axis=0,
        )
        product = sum(
            lax.dot_general(
                rows[128 * dy : 128 * dy + 512], taps_ref[dy], NT, preferred_element_type=F32
            )
            for dy in range(3)
        )
        pooled = jnp.concatenate(
            [product[0:128] + product[128:256], product[256:384] + product[384:512]], axis=0
        )
        after = jnp.where(column_high < 7, row_shift(pooled[:, 0:256], 1), 0.0)
        before = jnp.where(column_high > 0, row_shift(pooled[:, 512:768], -1), 0.0)
        moved = after + pooled[:, 256:512] + before
        moved = moved + row_shift(moved, 1)
        now, later = moved[:, 0:128], moved[:, 128:256]
        total = now
        total = total + jnp.where(frame < 15, row_shift(half_turn(now), 8), 0.0)
        total = total + jnp.where(frame < 14, row_shift(later, 16), 0.0)
        wide_ref[128 * pair : 128 * pair + 128, :] = jnp.where(
            low_half, total[0:128], half_turn(total[128:256])
        )
    summed = jnp.concatenate(
        [wide_ref[pl.ds(128 * pair, 64, stride=2), :] for pair in range(4)], axis=0
    )
    lane = iota((1, 128), 1)
    slot = (lane >> 3) & 7
    target = 128 * x + 16 * owner_z(slot, z, c) + 8 * c + (lane & 7)
    channel = iota((512, 128), 0)
    hit = channel == target
    half = iota((512, 128), 1) >> 6
    picks = [jnp.where(hit & (half == y), 1.0, 0.0).astype(BF16) for y in range(2)]
    mids = [
        jnp.concatenate([full_mid(edges_ref, 2 * pair + y) for pair in range(4)], axis=0)
        for y in range(2)
    ]
    mid = sum(
        jnp.dot(m, s, preferred_element_type=F32) for m, s in zip(mids, picks)
    )
    rms = [inverse_rms(m.astype(F32)) for m in mids]
    scaled = mid * jnp.where(iota((256, 128), 1) < 64, rms[0], rms[1])
    gain = jnp.dot(
        jnp.broadcast_to(gain_ref[...], (8, 512)),
        jnp.where(hit, 1.0, 0.0),
        precision=lax.Precision.HIGHEST,
        preferred_element_type=F32,
    )[0:1]
    normed = scaled * gain
    gate = jax.nn.sigmoid(normed)
    grad = summed * (gate * (1.0 + normed * (1.0 - gate)))
    sent = (grad * gain).astype(BF16)
    out_ref[...] = sent
    terms = jnp.sum(grad * scaled, axis=0, keepdims=True)
    terms = terms + half_turn(terms)
    source = iota((128, 128), 0)
    place = (source & 64) + 8 * owner_z((source >> 3) & 7, z, c) + (source & 7)
    order = jnp.where(place == iota((128, 128), 1), 1.0, 0.0)
    terms = jnp.dot(
        jnp.broadcast_to(terms, (8, 128)),
        order,
        precision=lax.Precision.HIGHEST,
        preferred_element_type=F32,
    )
    gain_out_ref[...] = terms


def low_kernel_body(
    place_ref, grads_ref, edges_ref, weight_ref, out_ref, turned_ref, taps_ref
):
    to, at = iota((144, 112), 0), iota((144, 112), 1)
    tap = 9 * (to // 48) + 3 * ((to >> 2) & 3) + (to >> 4) % 3
    pick = jnp.where((at == 4 * tap + (to & 3)) & (((to >> 2) & 3) < 3), 1.0, 0.0).astype(BF16)
    for n in range(8):
        taps_ref[n] = jnp.dot(
            pick, weight_ref[n, 0:112, :], preferred_element_type=F32
        ).astype(BF16)
    c, z = place_ref[1], place_ref[2]
    source = iota((256, 256), 0)
    target = (
        ((source >> 6) & 1) * 128
        + owner_z((source >> 3) & 7, z, source >> 7) * 16
        + (source >> 7) * 8
        + (source & 7)
    )
    order = jnp.where(target == iota((256, 256), 1), 1.0, 0.0).astype(BF16)
    placed = [
        jnp.dot(
            jnp.concatenate([grads_ref[2 * x], grads_ref[2 * x + 1]], axis=1),
            order,
            preferred_element_type=F32,
        )
        for x in range(4)
    ]
    halves = []
    for y in range(2):
        grad = jnp.concatenate([p[:, 128 * y : 128 * y + 128] for p in placed], axis=1)
        mid = jnp.concatenate(
            [full_mid(edges_ref, 2 * pair + y) for pair in range(4)], axis=0
        ).astype(F32)
        rms = inverse_rms(mid)
        scaled = mid * rms
        mean = jnp.mean(grad * scaled, axis=1, keepdims=True)
        halves.append((rms * (grad - scaled * mean)).astype(BF16))
    grads = jnp.concatenate(halves, axis=0)
    row = iota((512, 128), 0)
    frame = (row >> 2) & 15
    column = row & 3
    total = jnp.zeros((512, 128), F32)
    for a in range(3):
        for b in range(3):
            at = 16 * (3 * a + b)
            taps = jnp.concatenate([taps_ref[n, at : at + 16, :] for n in range(8)], axis=0)
            product = lax.dot_general(grads, taps, NT, preferred_element_type=F32)
            moved = row_shift(product, 4 * (2 - a) + 1 - b)
            keep = (frame + 2 - a < 16) & (column + 1 - b >= 0) & (column + 1 - b < 4)
            total = total + jnp.where(keep, moved, 0.0)
    result = total[0:256] + pltpu.roll(total[256:512], 4, 1)
    for pair in range(4):
        turned_ref[:, pair, :] = result[64 * pair : 64 * pair + 64]
    out_ref[...] = turned_ref[...].astype(BF16)


def close_body(rows_ref, terms_ref, out_ref):
    terms = terms_ref[0]
    for n in range(1, 4):
        terms = terms + terms_ref[n]
    head = terms.astype(BF16).astype(F32)
    line = jnp.where(iota((8, 128), 1) < 64, head, terms - head)[0:2].astype(BF16)
    out_ref[:, 0] = rows_ref[:, 0:2]
    out_ref[:, 1] = rows_ref[:, 2:4]
    out_ref[:, 2] = jnp.broadcast_to(line[None], (64, 2, 128))


def join_body(scale, parts_ref, out_ref, gain_ref, rows_ref):
    for n in range(3):
        rows_ref[:, 2 * n : 2 * n + 2, :] = parts_ref[:, n].astype(F32)
    rows_ref[:, 6:8, :] = jnp.zeros((64, 2, 128), F32)
    parts = rows_ref[...]
    strips = [
        jnp.concatenate([parts[16 * x + 2 * z + c] for z in range(8)], axis=0)
        for x in range(4)
        for c in range(2)
    ]
    wide = jnp.concatenate([s.astype(BF16) for s in strips], axis=1)
    lane = iota((64, 1024), 1)
    row_out = iota((64, 64), 0)
    row_in = iota((64, 64), 1)
    pair, z = row_in & 7, row_in >> 3
    joined = jnp.zeros((64, 1024), F32)
    for n in range(4):
        pick = (row_out == 16 * pair + 2 * z - 1 + n) & (pair < 4)
        placed = jnp.dot(
            jnp.where(pick, 1.0, 0.0).astype(BF16), wide, preferred_element_type=F32
        )
        joined = jnp.where(((lane >> 2) & 3) == n, placed, joined)
    source = iota((1024, 256), 0)
    target = (
        (source >> 8) * 64 + ((source >> 4) & 7) * 8 + ((source >> 7) & 1) * 4 + (source & 3)
    )
    order = jnp.where(target == iota((1024, 256), 1), 1.0, 0.0).astype(BF16)
    out_ref[...] = jnp.dot(
        joined.astype(BF16), order, preferred_element_type=F32
    ).astype(BF16)
    low_half = iota((1, 128), 1) < 64
    lines = []
    for x in range(4):
        pieces = []
        for c in range(2):
            piece = sum(parts[16 * x + 2 * z + c, 4:5, :] for z in range(8))
            pieces.append(piece + half_turn(piece))
        lines.append(jnp.where(low_half, pieces[0], pieces[1]))
    lines = jnp.concatenate(lines + lines, axis=0)
    source = iota((128, 128), 0)
    target = ((source >> 3) & 7) * 16 + (source >> 6) * 8 + (source & 7)
    order = jnp.where(target == iota((128, 128), 1), 1.0, 0.0)
    gain_ref[...] = (
        jnp.dot(lines, order, precision=lax.Precision.HIGHEST, preferred_element_type=F32)[0:4]
        * scale
    )


def whole():
    return pl.BlockSpec(memory_space=pltpu.VMEM)


def scalars():
    return pl.BlockSpec(memory_space=pltpu.SMEM)


PARAMS = pltpu.CompilerParams(vmem_limit_bytes=40 * 1024 * 1024)


def ring_pairs(distances):
    pairs = []
    for zh in range(2):
        for y in range(4):
            for zl in range(8):
                for c in range(2):
                    at = (zh * 8 + zl + distances[c][y]) % 16
                    source = ((at // 8 * 4 + y) * 8 + at % 8) * 2 + c
                    pairs.append((source, ((zh * 4 + y) * 8 + zl) * 2 + c))
    return pairs


def shards(grad_out, saved_mid, norm_gain, high_kernel, low_kernel):
    x, z, c = (lax.axis_index(n) for n in ("x", "zl", "c"))
    place = jnp.stack([x, c, z]).astype(jnp.int32)
    ring = ("zh", "y", "zl", "c")
    group = ("x", "c")
    shard = ("x", "zl", "c")

    grad = grad_out[0]
    own = jnp.transpose(grad, (1, 0, 2, 3)).reshape(256, 256)
    halo_pairs = [(s, s - 1) for s in range(2, 64, 2)] + [(s, s + 1) for s in range(1, 62, 2)]
    halo = lax.ppermute(own, shard, halo_pairs)

    high = jnp.transpose(high_kernel, (1, 0, 2))
    near = lax.ppermute(high, ring, ring_pairs(NEAR))
    far = lax.ppermute(high, ring, ring_pairs(FAR))
    low = jnp.pad(jnp.transpose(low_kernel, (1, 0, 2)).reshape(108, 512), ((0, 20), (0, 0)))
    low_all = lax.all_gather(low, "zl", axis=0)

    def spread(block):
        return lax.all_to_all(
            jnp.broadcast_to(block[None], (8, 256, 256)), group, split_axis=0, concat_axis=0, tiled=True
        )

    parts = spread(own)
    mid = saved_mid.reshape(64, 512)
    halo, parts, near, far = lax.optimization_barrier((halo, parts, near, far))
    halo = jnp.where(c == 0, halo[128:256], halo[0:128])
    edges = spread(jnp.concatenate([halo, mid[:, 0:256], mid[:, 256:512]], axis=0))
    high = jnp.concatenate([near, far], axis=1)
    high_all = lax.all_gather(high.reshape(432, 256), "y", axis=0)
    grads, gain_terms = pl.pallas_call(
        high_kernel_body,
        out_shape=(
            jax.ShapeDtypeStruct((256, 128), BF16),
            jax.ShapeDtypeStruct((8, 128), F32),
        ),
        in_specs=[scalars()] + [whole()] * 4,
        out_specs=(whole(), whole()),
        scratch_shapes=[pltpu.VMEM((3, 768, 256), BF16), pltpu.VMEM((512, 128), F32)],
        compiler_params=PARAMS,
        name="high_conv",
    )(place, parts, edges, high_all, norm_gain.reshape(1, 512))

    halves = [(z, (z + 4) % 16 if z % 8 >= 4 else (z - 4) % 16) for z in range(16)]
    other = lax.ppermute(gain_terms, ("zh", "zl"), halves)
    gathered = lax.all_gather(grads, group, axis=0)
    other, gathered = lax.optimization_barrier((other, gathered))
    clips = lax.all_to_all(
        jnp.broadcast_to((gain_terms + other)[None], (4, 8, 128)), "y", split_axis=0, concat_axis=0, tiled=True
    )

    partial = pl.pallas_call(
        low_kernel_body,
        out_shape=jax.ShapeDtypeStruct((64, 4, 128), BF16),
        in_specs=[scalars(), whole(), whole(), whole()],
        out_specs=whole(),
        scratch_shapes=[pltpu.VMEM((64, 4, 128), F32), pltpu.VMEM((8, 144, 512), BF16)],
        compiler_params=PARAMS,
        name="low_conv",
    )(place, gathered, edges, low_all)

    outgoing = pl.pallas_call(
        close_body,
        out_shape=jax.ShapeDtypeStruct((64, 3, 2, 128), BF16),
        in_specs=[whole(), whole()],
        out_specs=whole(),
        compiler_params=PARAMS,
        name="close",
    )(partial, clips)
    outgoing = outgoing.reshape(192, 2, 128)
    incoming = lax.all_to_all(outgoing, shard, split_axis=0, concat_axis=0, tiled=True)

    positions = 8 * 16 * 128 * 8
    grad_in, gain_grad = pl.pallas_call(
        lambda *refs: join_body(1.0 / math.sqrt(positions), *refs),
        out_shape=(
            jax.ShapeDtypeStruct((64, 256), BF16),
            jax.ShapeDtypeStruct((4, 128), F32),
        ),
        in_specs=[whole()],
        out_specs=(whole(), whole()),
        scratch_shapes=[pltpu.VMEM((64, 8, 128), F32)],
        compiler_params=PARAMS,
        name="join",
    )(incoming.reshape(64, 3, 2, 128))
    return (grad_in.reshape(1, 1, 64, 1, 256), gain_grad.reshape(512))


def solution(mesh):
    fine = Mesh(mesh.devices.reshape(2, 4, 4, 8, 2), ("zh", "y", "x", "zl", "c"))
    dp, shard = ("zh", "y"), ("x", "zl", "c")
    return jax.shard_map(
        shards,
        mesh=fine,
        in_specs=(
            P(dp, None, shard, None, None),
            P(dp, None, shard, None, None),
            P(),
            P(shard, None, None),
            P(shard, None, None),
        ),
        out_specs=(P(dp, shard, None, None, None), P()),
        check_vma=False,
    )
```

```python
import math

import jax
import jax.numpy as jnp
from jax import lax
from jax.experimental import pallas as pl
from jax.experimental.pallas import tpu as pltpu
from jax.sharding import Mesh
from jax.sharding import PartitionSpec as P

EPSILON = 1e-06
F32 = jnp.float32
BF16 = jnp.bfloat16
NEAR = ((0, 1, -1, 2), (0, -1, 1, 2))
FAR = ((4, -3, 3, -2), (-4, 3, -3, -2))
NT = (((1,), (1,)), ((), ()))


def iota(shape, dim):
    return lax.broadcasted_iota(jnp.int32, shape, dim)


def owner_z(slot, z, c):
    offset = jnp.zeros_like(slot)
    for y in range(4):
        for n, table in enumerate((NEAR, FAR)):
            by = jnp.where(c == 0, table[0][y] % 8, table[1][y] % 8)
            offset = jnp.where(slot == 2 * y + n, by, offset)
    return (z + offset) & 7


def slot_of(owner, z, c):
    distance = (owner - z) & 7
    slot = jnp.int32(0)
    for y in range(4):
        for n, table in enumerate((NEAR, FAR)):
            by = jnp.where(c == 0, table[0][y] % 8, table[1][y] % 8)
            slot = jnp.where(distance == by, 2 * y + n, slot)
    return slot


def row_shift(value, by):
    rows = value.shape[0]
    by = by % rows
    return value if by == 0 else pltpu.roll(value, rows - by, 0)


def half_turn(value):
    return pltpu.roll(value, 64, 1)


def full_mid(edges_ref, source):
    return jnp.concatenate(
        [edges_ref[source, 128:192, :], edges_ref[source, 192:256, :]], axis=1
    )


def inverse_rms(mid):
    return lax.rsqrt(jnp.mean(mid * mid, axis=1, keepdims=True) + EPSILON)


def high_kernel_body(place_ref, parts_ref, edges_ref, weight_ref, gain_ref, out_ref, gain_out_ref, taps_ref, wide_ref):
    x, c, z = place_ref[0], place_ref[1], place_ref[2]
    for dy in range(3):
        for dw in range(3):
            for dt in range(3):
                tap = 9 * (2 - dt) + 3 * (2 - dy) + dw
                for j in range(4):
                    at = (dw * 4 + dt) * 64 + 16 * j
                    taps_ref[dy, at : at + 16, :] = weight_ref[j, 16 * tap : 16 * tap + 16, :]
            at = (dw * 4 + 3) * 64
            taps_ref[dy, at : at + 64, :] = jnp.zeros((64, 256), BF16)
    row = iota((256, 256), 0)
    column_high = row & 7
    frame = (iota((256, 128), 0) >> 3) & 15
    low_half = iota((128, 128), 1) < 64
    for pair in range(4):
        rows = jnp.concatenate(
            [
                edges_ref[2 * pair, 0:128, :],
                parts_ref[2 * pair],
                parts_ref[2 * pair + 1],
                edges_ref[2 * pair + 1, 0:128, :],
            ],
            axis=0,
        )
        product = sum(
            lax.dot_general(
                rows[128 * dy : 128 * dy + 512], taps_ref[dy], NT, preferred_element_type=F32
            )
            for dy in range(3)
        )
        pooled = jnp.concatenate(
            [product[0:128] + product[128:256], product[256:384] + product[384:512]], axis=0
        )
        after = jnp.where(column_high < 7, row_shift(pooled[:, 0:256], 1), 0.0)
        before = jnp.where(column_high > 0, row_shift(pooled[:, 512:768], -1), 0.0)
        moved = after + pooled[:, 256:512] + before
        moved = moved + row_shift(moved, 1)
        now, later = moved[:, 0:128], moved[:, 128:256]
        total = now
        total = total + jnp.where(frame < 15, row_shift(half_turn(now), 8), 0.0)
        total = total + jnp.where(frame < 14, row_shift(later, 16), 0.0)
        wide_ref[128 * pair : 128 * pair + 128, :] = jnp.where(
            low_half, total[0:128], half_turn(total[128:256])
        )
    summed = jnp.concatenate(
        [wide_ref[pl.ds(128 * pair, 64, stride=2), :] for pair in range(4)], axis=0
    )
    lane = iota((1, 128), 1)
    slot = (lane >> 3) & 7
    target = 128 * x + 16 * owner_z(slot, z, c) + 8 * c + (lane & 7)
    channel = iota((512, 128), 0)
    hit = channel == target
    half = iota((512, 128), 1) >> 6
    picks = [jnp.where(hit & (half == y), 1.0, 0.0).astype(BF16) for y in range(2)]
    mids = [
        jnp.concatenate([full_mid(edges_ref, 2 * pair + y) for pair in range(4)], axis=0)
        for y in range(2)
    ]
    mid = sum(
        jnp.dot(m, s, preferred_element_type=F32) for m, s in zip(mids, picks)
    )
    rms = [inverse_rms(m.astype(F32)) for m in mids]
    scaled = mid * jnp.where(iota((256, 128), 1) < 64, rms[0], rms[1])
    gain = jnp.dot(
        jnp.broadcast_to(gain_ref[...], (8, 512)),
        jnp.where(hit, 1.0, 0.0),
        precision=lax.Precision.HIGHEST,
        preferred_element_type=F32,
    )[0:1]
    normed = scaled * gain
    gate = jax.nn.sigmoid(normed)
    grad = summed * (gate * (1.0 + normed * (1.0 - gate)))
    sent = (grad * gain).astype(BF16)
    out_ref[...] = sent
    terms = jnp.sum(grad * scaled, axis=0, keepdims=True)
    terms = terms + half_turn(terms)
    source = iota((128, 128), 0)
    place = (source & 64) + 8 * owner_z((source >> 3) & 7, z, c) + (source & 7)
    order = jnp.where(place == iota((128, 128), 1), 1.0, 0.0)
    terms = jnp.dot(
        jnp.broadcast_to(terms, (8, 128)),
        order,
        precision=lax.Precision.HIGHEST,
        preferred_element_type=F32,
    )
    gain_out_ref[...] = terms


def low_kernel_body(
    place_ref, grads_ref, edges_ref, weight_ref, out_ref, taps_ref
):
    to, at = iota((144, 112), 0), iota((144, 112), 1)
    tap = 9 * (to // 48) + 3 * ((to >> 2) & 3) + (to >> 4) % 3
    pick = jnp.where((at == 4 * tap + (to & 3)) & (((to >> 2) & 3) < 3), 1.0, 0.0).astype(BF16)
    for n in range(8):
        taps_ref[n] = jnp.dot(
            pick, weight_ref[n, 0:112, :], preferred_element_type=F32
        ).astype(BF16)
    c, z = place_ref[1], place_ref[2]
    source = iota((256, 256), 0)
    target = (
        ((source >> 6) & 1) * 128
        + owner_z((source >> 3) & 7, z, source >> 7) * 16
        + (source >> 7) * 8
        + (source & 7)
    )
    order = jnp.where(target == iota((256, 256), 1), 1.0, 0.0).astype(BF16)
    placed = [
        jnp.dot(
            jnp.concatenate([grads_ref[2 * x], grads_ref[2 * x + 1]], axis=1),
            order,
            preferred_element_type=F32,
        )
        for x in range(4)
    ]
    halves = []
    for y in range(2):
        grad = jnp.concatenate([p[:, 128 * y : 128 * y + 128] for p in placed], axis=1)
        mid = jnp.concatenate(
            [full_mid(edges_ref, 2 * pair + y) for pair in range(4)], axis=0
        ).astype(F32)
        rms = inverse_rms(mid)
        scaled = mid * rms
        mean = jnp.mean(grad * scaled, axis=1, keepdims=True)
        halves.append((rms * (grad - scaled * mean)).astype(BF16))
    grads = jnp.concatenate(halves, axis=0)
    row = iota((512, 128), 0)
    frame = (row >> 2) & 15
    column = row & 3
    total = jnp.zeros((512, 128), F32)
    for a in range(3):
        for b in range(3):
            at = 16 * (3 * a + b)
            taps = jnp.concatenate([taps_ref[n, at : at + 16, :] for n in range(8)], axis=0)
            product = lax.dot_general(grads, taps, NT, preferred_element_type=F32)
            moved = row_shift(product, 4 * (2 - a) + 1 - b)
            keep = (frame + 2 - a < 16) & (column + 1 - b >= 0) & (column + 1 - b < 4)
            total = total + jnp.where(keep, moved, 0.0)
    result = total[0:256] + pltpu.roll(total[256:512], 4, 1)
    for pair in range(4):
        out_ref[:, pair, :] = result[64 * pair : 64 * pair + 64]


def close_body(rows_ref, terms_ref, out_ref):
    terms = terms_ref[0]
    for n in range(1, 4):
        terms = terms + terms_ref[n]
    head = terms.astype(BF16).astype(F32)
    line = jnp.where(iota((8, 128), 1) < 64, head, terms - head)[0:2].astype(BF16)
    out_ref[:, 0] = rows_ref[:, 0:2].astype(BF16)
    out_ref[:, 1] = rows_ref[:, 2:4].astype(BF16)
    out_ref[:, 2] = jnp.broadcast_to(line[None], (64, 2, 128))


def join_body(scale, parts_ref, out_ref, gain_ref, rows_ref):
    for n in range(3):
        rows_ref[:, 2 * n : 2 * n + 2, :] = parts_ref[:, n].astype(F32)
    rows_ref[:, 6:8, :] = jnp.zeros((64, 2, 128), F32)
    parts = rows_ref[...]
    strips = [
        jnp.concatenate([parts[16 * x + 2 * z + c] for z in range(8)], axis=0)
        for x in range(4)
        for c in range(2)
    ]
    wide = jnp.concatenate([s.astype(BF16) for s in strips], axis=1)
    lane = iota((64, 1024), 1)
    row_out = iota((64, 64), 0)
    row_in = iota((64, 64), 1)
    pair, z = row_in & 7, row_in >> 3
    joined = jnp.zeros((64, 1024), F32)
    for n in range(4):
        pick = (row_out == 16 * pair + 2 * z - 1 + n) & (pair < 4)
        placed = jnp.dot(
            jnp.where(pick, 1.0, 0.0).astype(BF16), wide, preferred_element_type=F32
        )
        joined = jnp.where(((lane >> 2) & 3) == n, placed, joined)
    source = iota((1024, 256), 0)
    target = (
        (source >> 8) * 64 + ((source >> 4) & 7) * 8 + ((source >> 7) & 1) * 4 + (source & 3)
    )
    order = jnp.where(target == iota((1024, 256), 1), 1.0, 0.0).astype(BF16)
    out_ref[...] = jnp.dot(
        joined.astype(BF16), order, preferred_element_type=F32
    ).astype(BF16)
    low_half = iota((1, 128), 1) < 64
    lines = []
    for x in range(4):
        pieces = []
        for c in range(2):
            piece = sum(parts[16 * x + 2 * z + c, 4:5, :] for z in range(8))
            pieces.append(piece + half_turn(piece))
        lines.append(jnp.where(low_half, pieces[0], pieces[1]))
    lines = jnp.concatenate(lines + lines, axis=0)
    source = iota((128, 128), 0)
    target = ((source >> 3) & 7) * 16 + (source >> 6) * 8 + (source & 7)
    order = jnp.where(target == iota((128, 128), 1), 1.0, 0.0)
    gain_ref[...] = (
        jnp.dot(lines, order, precision=lax.Precision.HIGHEST, preferred_element_type=F32)[0:4]
        * scale
    )


def whole():
    return pl.BlockSpec(memory_space=pltpu.VMEM)


def scalars():
    return pl.BlockSpec(memory_space=pltpu.SMEM)


PARAMS = pltpu.CompilerParams(vmem_limit_bytes=40 * 1024 * 1024)


def ring_pairs(distances):
    pairs = []
    for zh in range(2):
        for y in range(4):
            for zl in range(8):
                for c in range(2):
                    at = (zh * 8 + zl + distances[c][y]) % 16
                    source = ((at // 8 * 4 + y) * 8 + at % 8) * 2 + c
                    pairs.append((source, ((zh * 4 + y) * 8 + zl) * 2 + c))
    return pairs


def shards(grad_out, saved_mid, norm_gain, high_kernel, low_kernel):
    x, z, c = (lax.axis_index(n) for n in ("x", "zl", "c"))
    place = jnp.stack([x, c, z]).astype(jnp.int32)
    ring = ("zh", "y", "zl", "c")
    group = ("x", "c")
    shard = ("x", "zl", "c")

    grad = grad_out[0]
    own = jnp.transpose(grad, (1, 0, 2, 3)).reshape(256, 256)
    halo_pairs = [(s, s - 1) for s in range(2, 64, 2)] + [(s, s + 1) for s in range(1, 62, 2)]
    halo = lax.ppermute(own, shard, halo_pairs)

    high = jnp.transpose(high_kernel, (1, 0, 2))
    near = lax.ppermute(high, ring, ring_pairs(NEAR))
    far = lax.ppermute(high, ring, ring_pairs(FAR))
    low = jnp.pad(jnp.transpose(low_kernel, (1, 0, 2)).reshape(108, 512), ((0, 20), (0, 0)))
    low_all = lax.all_gather(low, "zl", axis=0)

    def spread(block):
        return lax.all_to_all(
            jnp.broadcast_to(block[None], (8, 256, 256)), group, split_axis=0, concat_axis=0, tiled=True
        )

    parts = spread(own)
    mid = saved_mid.reshape(64, 512)
    halo, parts, near, far = lax.optimization_barrier((halo, parts, near, far))
    halo = jnp.where(c == 0, halo[128:256], halo[0:128])
    edges = spread(jnp.concatenate([halo, mid[:, 0:256], mid[:, 256:512]], axis=0))
    high = jnp.concatenate([near, far], axis=1)
    high_all = lax.all_gather(high.reshape(432, 256), "y", axis=0)
    grads, gain_terms = pl.pallas_call(
        high_kernel_body,
        out_shape=(
            jax.ShapeDtypeStruct((256, 128), BF16),
            jax.ShapeDtypeStruct((8, 128), F32),
        ),
        in_specs=[scalars()] + [whole()] * 4,
        out_specs=(whole(), whole()),
        scratch_shapes=[pltpu.VMEM((3, 768, 256), BF16), pltpu.VMEM((512, 128), F32)],
        compiler_params=PARAMS,
        name="high_conv",
    )(place, parts, edges, high_all, norm_gain.reshape(1, 512))

    halves = [(z, (z + 4) % 16 if z % 8 >= 4 else (z - 4) % 16) for z in range(16)]
    other = lax.ppermute(gain_terms, ("zh", "zl"), halves)
    gathered = lax.all_gather(grads, group, axis=0)
    other, gathered = lax.optimization_barrier((other, gathered))
    clips = lax.all_to_all(
        jnp.broadcast_to((gain_terms + other)[None], (4, 8, 128)), "y", split_axis=0, concat_axis=0, tiled=True
    )

    partial = pl.pallas_call(
        low_kernel_body,
        out_shape=jax.ShapeDtypeStruct((64, 4, 128), F32),
        in_specs=[scalars(), whole(), whole(), whole()],
        out_specs=whole(),
        scratch_shapes=[pltpu.VMEM((8, 144, 512), BF16)],
        compiler_params=PARAMS,
        name="low_conv",
    )(place, gathered, edges, low_all)

    outgoing = pl.pallas_call(
        close_body,
        out_shape=jax.ShapeDtypeStruct((64, 3, 2, 128), BF16),
        in_specs=[whole(), whole()],
        out_specs=whole(),
        compiler_params=PARAMS,
        name="close",
    )(partial, clips)
    outgoing = outgoing.reshape(192, 2, 128)
    incoming = lax.all_to_all(outgoing, shard, split_axis=0, concat_axis=0, tiled=True)

    positions = 8 * 16 * 128 * 8
    grad_in, gain_grad = pl.pallas_call(
        lambda *refs: join_body(1.0 / math.sqrt(positions), *refs),
        out_shape=(
            jax.ShapeDtypeStruct((64, 256), BF16),
            jax.ShapeDtypeStruct((4, 128), F32),
        ),
        in_specs=[whole()],
        out_specs=(whole(), whole()),
        scratch_shapes=[pltpu.VMEM((64, 8, 128), F32)],
        compiler_params=PARAMS,
        name="join",
    )(incoming.reshape(64, 3, 2, 128))
    return (grad_in.reshape(1, 1, 64, 1, 256), gain_grad.reshape(512))


def solution(mesh):
    fine = Mesh(mesh.devices.reshape(2, 4, 4, 8, 2), ("zh", "y", "x", "zl", "c"))
    dp, shard = ("zh", "y"), ("x", "zl", "c")
    return jax.shard_map(
        shards,
        mesh=fine,
        in_specs=(
            P(dp, None, shard, None, None),
            P(dp, None, shard, None, None),
            P(),
            P(shard, None, None),
            P(shard, None, None),
        ),
        out_specs=(P(dp, shard, None, None, None), P()),
        check_vma=False,
    )
```

```python
import math

import jax
import jax.numpy as jnp
from jax import lax
from jax.experimental import pallas as pl
from jax.experimental.pallas import tpu as pltpu
from jax.sharding import Mesh
from jax.sharding import PartitionSpec as P

EPSILON = 1e-06
F32 = jnp.float32
BF16 = jnp.bfloat16
NEAR = ((0, 1, -1, 2), (0, -1, 1, 2))
FAR = ((4, -3, 3, -2), (-4, 3, -3, -2))
NT = (((1,), (1,)), ((), ()))


def iota(shape, dim):
    return lax.broadcasted_iota(jnp.int32, shape, dim)


def owner_z(slot, z, c):
    offset = jnp.zeros_like(slot)
    for y in range(4):
        for n, table in enumerate((NEAR, FAR)):
            by = jnp.where(c == 0, table[0][y] % 8, table[1][y] % 8)
            offset = jnp.where(slot == 2 * y + n, by, offset)
    return (z + offset) & 7


def slot_of(owner, z, c):
    distance = (owner - z) & 7
    slot = jnp.int32(0)
    for y in range(4):
        for n, table in enumerate((NEAR, FAR)):
            by = jnp.where(c == 0, table[0][y] % 8, table[1][y] % 8)
            slot = jnp.where(distance == by, 2 * y + n, slot)
    return slot


def row_shift(value, by):
    rows = value.shape[0]
    by = by % rows
    return value if by == 0 else pltpu.roll(value, rows - by, 0)


def half_turn(value):
    return pltpu.roll(value, 64, 1)


def full_mid(edges_ref, source):
    return jnp.concatenate(
        [edges_ref[source, 128:192, :], edges_ref[source, 192:256, :]], axis=1
    )


def inverse_rms(mid):
    return lax.rsqrt(jnp.mean(mid * mid, axis=1, keepdims=True) + EPSILON)


def high_kernel_body(place_ref, parts_ref, edges_ref, weight_ref, gain_ref, out_ref, gain_out_ref, taps_ref, wide_ref):
    x, c, z = place_ref[0], place_ref[1], place_ref[2]
    for dy in range(3):
        for dw in range(3):
            for dt in range(3):
                tap = 9 * (2 - dt) + 3 * (2 - dy) + dw
                for j in range(4):
                    at = (dw * 4 + dt) * 64 + 16 * j
                    taps_ref[dy, at : at + 16, :] = weight_ref[j, 16 * tap : 16 * tap + 16, :]
            at = (dw * 4 + 3) * 64
            taps_ref[dy, at : at + 64, :] = jnp.zeros((64, 256), BF16)
    row = iota((256, 256), 0)
    column_high = row & 7
    frame = (iota((256, 128), 0) >> 3) & 15
    low_half = iota((128, 128), 1) < 64
    for pair in range(4):
        rows = jnp.concatenate(
            [
                edges_ref[2 * pair, 0:128, :],
                parts_ref[2 * pair],
                parts_ref[2 * pair + 1],
                edges_ref[2 * pair + 1, 0:128, :],
            ],
            axis=0,
        )
        product = sum(
            lax.dot_general(
                rows[128 * dy : 128 * dy + 512], taps_ref[dy], NT, preferred_element_type=F32
            )
            for dy in range(3)
        )
        pooled = jnp.concatenate(
            [product[0:128] + product[128:256], product[256:384] + product[384:512]], axis=0
        )
        after = jnp.where(column_high < 7, row_shift(pooled[:, 0:256], 1), 0.0)
        before = jnp.where(column_high > 0, row_shift(pooled[:, 512:768], -1), 0.0)
        moved = after + pooled[:, 256:512] + before
        moved = moved + row_shift(moved, 1)
        now, later = moved[:, 0:128], moved[:, 128:256]
        total = now
        total = total + jnp.where(frame < 15, row_shift(half_turn(now), 8), 0.0)
        total = total + jnp.where(frame < 14, row_shift(later, 16), 0.0)
        wide_ref[128 * pair : 128 * pair + 128, :] = jnp.where(
            low_half, total[0:128], half_turn(total[128:256])
        )
    summed = jnp.concatenate(
        [wide_ref[pl.ds(128 * pair, 64, stride=2), :] for pair in range(4)], axis=0
    )
    lane = iota((1, 128), 1)
    slot = (lane >> 3) & 7
    target = 128 * x + 16 * owner_z(slot, z, c) + 8 * c + (lane & 7)
    channel = iota((512, 128), 0)
    hit = channel == target
    half = iota((512, 128), 1) >> 6
    picks = [jnp.where(hit & (half == y), 1.0, 0.0).astype(BF16) for y in range(2)]
    mids = [
        jnp.concatenate([full_mid(edges_ref, 2 * pair + y) for pair in range(4)], axis=0)
        for y in range(2)
    ]
    mid = sum(
        jnp.dot(m, s, preferred_element_type=F32) for m, s in zip(mids, picks)
    )
    rms = [inverse_rms(m.astype(F32)) for m in mids]
    scaled = mid * jnp.where(iota((256, 128), 1) < 64, rms[0], rms[1])
    gain = jnp.dot(
        jnp.broadcast_to(gain_ref[...], (8, 512)),
        jnp.where(hit, 1.0, 0.0),
        precision=lax.Precision.HIGHEST,
        preferred_element_type=F32,
    )[0:1]
    normed = scaled * gain
    gate = jax.nn.sigmoid(normed)
    grad = summed * (gate * (1.0 + normed * (1.0 - gate)))
    sent = (grad * gain).astype(BF16)
    out_ref[...] = sent
    terms = jnp.sum(grad * scaled, axis=0, keepdims=True)
    terms = terms + half_turn(terms)
    source = iota((128, 128), 0)
    place = (source & 64) + 8 * owner_z((source >> 3) & 7, z, c) + (source & 7)
    order = jnp.where(place == iota((128, 128), 1), 1.0, 0.0)
    terms = jnp.dot(
        jnp.broadcast_to(terms, (8, 128)),
        order,
        precision=lax.Precision.HIGHEST,
        preferred_element_type=F32,
    )
    for n in range(4):
        gain_out_ref[n] = terms


def norm_body(place_ref, grads_ref, edges_ref, out_ref):
    c, z = place_ref[1], place_ref[2]
    source = iota((256, 256), 0)
    target = (
        ((source >> 6) & 1) * 128
        + owner_z((source >> 3) & 7, z, source >> 7) * 16
        + (source >> 7) * 8
        + (source & 7)
    )
    order = jnp.where(target == iota((256, 256), 1), 1.0, 0.0).astype(BF16)
    placed = [
        jnp.dot(
            jnp.concatenate([grads_ref[2 * x], grads_ref[2 * x + 1]], axis=1),
            order,
            preferred_element_type=F32,
        )
        for x in range(4)
    ]
    halves = []
    for y in range(2):
        grad = jnp.concatenate([p[:, 128 * y : 128 * y + 128] for p in placed], axis=1)
        mid = jnp.concatenate(
            [full_mid(edges_ref, 2 * pair + y) for pair in range(4)], axis=0
        ).astype(F32)
        rms = inverse_rms(mid)
        scaled = mid * rms
        mean = jnp.mean(grad * scaled, axis=1, keepdims=True)
        halves.append((rms * (grad - scaled * mean)).astype(BF16))
    out_ref[...] = jnp.concatenate(halves, axis=0)


def low_kernel_body(grads_ref, weight_ref, out_ref, taps_ref):
    to, at = iota((144, 112), 0), iota((144, 112), 1)
    tap = 9 * (to // 48) + 3 * ((to >> 2) & 3) + (to >> 4) % 3
    pick = jnp.where((at == 4 * tap + (to & 3)) & (((to >> 2) & 3) < 3), 1.0, 0.0).astype(BF16)
    for n in range(8):
        taps_ref[n] = jnp.dot(
            pick, weight_ref[n, 0:112, :], preferred_element_type=F32
        ).astype(BF16)
    grads = grads_ref[...]
    row = iota((512, 128), 0)
    frame = (row >> 2) & 15
    column = row & 3
    total = jnp.zeros((512, 128), F32)
    for a in range(3):
        for b in range(3):
            at = 16 * (3 * a + b)
            taps = jnp.concatenate([taps_ref[n, at : at + 16, :] for n in range(8)], axis=0)
            product = lax.dot_general(grads, taps, NT, preferred_element_type=F32)
            moved = row_shift(product, 4 * (2 - a) + 1 - b)
            keep = (frame + 2 - a < 16) & (column + 1 - b >= 0) & (column + 1 - b < 4)
            total = total + jnp.where(keep, moved, 0.0)
    result = total[0:256] + pltpu.roll(total[256:512], 4, 1)
    for pair in range(4):
        out_ref[:, pair, :] = result[64 * pair : 64 * pair + 64]


def close_body(rows_ref, terms_ref, out_ref):
    terms = terms_ref[0]
    for n in range(1, 4):
        terms = terms + terms_ref[n]
    head = terms.astype(BF16).astype(F32)
    line = jnp.where(iota((8, 128), 1) < 64, head, terms - head)[0:2].astype(BF16)
    out_ref[:, 0] = rows_ref[:, 0:2].astype(BF16)
    out_ref[:, 1] = rows_ref[:, 2:4].astype(BF16)
    out_ref[:, 2] = jnp.broadcast_to(line[None], (64, 2, 128))


def join_body(scale, parts_ref, out_ref, gain_ref, rows_ref):
    for n in range(3):
        rows_ref[:, 2 * n : 2 * n + 2, :] = parts_ref[:, n].astype(F32)
    rows_ref[:, 6:8, :] = jnp.zeros((64, 2, 128), F32)
    parts = rows_ref[...]
    strips = [
        jnp.concatenate([parts[16 * x + 2 * z + c] for z in range(8)], axis=0)
        for x in range(4)
        for c in range(2)
    ]
    wide = jnp.concatenate([s.astype(BF16) for s in strips], axis=1)
    lane = iota((64, 1024), 1)
    row_out = iota((64, 64), 0)
    row_in = iota((64, 64), 1)
    pair, z = row_in & 7, row_in >> 3
    joined = jnp.zeros((64, 1024), F32)
    for n in range(4):
        pick = (row_out == 16 * pair + 2 * z - 1 + n) & (pair < 4)
        placed = jnp.dot(
            jnp.where(pick, 1.0, 0.0).astype(BF16), wide, preferred_element_type=F32
        )
        joined = jnp.where(((lane >> 2) & 3) == n, placed, joined)
    source = iota((1024, 256), 0)
    target = (
        (source >> 8) * 64 + ((source >> 4) & 7) * 8 + ((source >> 7) & 1) * 4 + (source & 3)
    )
    order = jnp.where(target == iota((1024, 256), 1), 1.0, 0.0).astype(BF16)
    out_ref[...] = jnp.dot(
        joined.astype(BF16), order, preferred_element_type=F32
    ).astype(BF16)
    low_half = iota((1, 128), 1) < 64
    lines = []
    for x in range(4):
        pieces = []
        for c in range(2):
            piece = sum(parts[16 * x + 2 * z + c, 4:5, :] for z in range(8))
            pieces.append(piece + half_turn(piece))
        lines.append(jnp.where(low_half, pieces[0], pieces[1]))
    lines = jnp.concatenate(lines + lines, axis=0)
    source = iota((128, 128), 0)
    target = ((source >> 3) & 7) * 16 + (source >> 6) * 8 + (source & 7)
    order = jnp.where(target == iota((128, 128), 1), 1.0, 0.0)
    gain_ref[...] = (
        jnp.dot(lines, order, precision=lax.Precision.HIGHEST, preferred_element_type=F32)[0:4]
        * scale
    )


def whole():
    return pl.BlockSpec(memory_space=pltpu.VMEM)


def scalars():
    return pl.BlockSpec(memory_space=pltpu.SMEM)


PARAMS = pltpu.CompilerParams(vmem_limit_bytes=40 * 1024 * 1024)


def ring_pairs(distances):
    pairs = []
    for zh in range(2):
        for y in range(4):
            for zl in range(8):
                for c in range(2):
                    at = (zh * 8 + zl + distances[c][y]) % 16
                    source = ((at // 8 * 4 + y) * 8 + at % 8) * 2 + c
                    pairs.append((source, ((zh * 4 + y) * 8 + zl) * 2 + c))
    return pairs


def shards(grad_out, saved_mid, norm_gain, high_kernel, low_kernel):
    x, z, c = (lax.axis_index(n) for n in ("x", "zl", "c"))
    place = jnp.stack([x, c, z]).astype(jnp.int32)
    ring = ("zh", "y", "zl", "c")
    group = ("x", "c")
    shard = ("x", "zl", "c")

    grad = grad_out[0]
    own = jnp.transpose(grad, (1, 0, 2, 3)).reshape(256, 256)
    halo_pairs = [(s, s - 1) for s in range(2, 64, 2)] + [(s, s + 1) for s in range(1, 62, 2)]
    halo = lax.ppermute(own, shard, halo_pairs)

    high = jnp.transpose(high_kernel, (1, 0, 2))
    near = lax.ppermute(high, ring, ring_pairs(NEAR))
    far = lax.ppermute(high, ring, ring_pairs(FAR))
    low = jnp.pad(jnp.transpose(low_kernel, (1, 0, 2)).reshape(108, 512), ((0, 20), (0, 0)))
    low_all = lax.all_gather(low, "zl", axis=0)

    def spread(block):
        return lax.all_to_all(
            jnp.broadcast_to(block[None], (8, 256, 256)), group, split_axis=0, concat_axis=0, tiled=True
        )

    parts = spread(own)
    mid = saved_mid.reshape(64, 512)
    halo, parts, near, far = lax.optimization_barrier((halo, parts, near, far))
    halo = jnp.where(c == 0, halo[128:256], halo[0:128])
    edges = spread(jnp.concatenate([halo, mid[:, 0:256], mid[:, 256:512]], axis=0))
    high = jnp.concatenate([near, far], axis=1)
    high_all = lax.all_gather(high.reshape(432, 256), "y", axis=0)
    grads, gain_terms = pl.pallas_call(
        high_kernel_body,
        out_shape=(
            jax.ShapeDtypeStruct((256, 128), BF16),
            jax.ShapeDtypeStruct((4, 8, 128), F32),
        ),
        in_specs=[scalars()] + [whole()] * 4,
        out_specs=(whole(), whole()),
        scratch_shapes=[pltpu.VMEM((3, 768, 256), BF16), pltpu.VMEM((512, 128), F32)],
        compiler_params=PARAMS,
        name="high_conv",
    )(place, parts, edges, high_all, norm_gain.reshape(1, 512))

    halves = [(z, (z + 4) % 16 if z % 8 >= 4 else (z - 4) % 16) for z in range(16)]
    other = lax.ppermute(gain_terms, ("zh", "zl"), halves)
    gathered = lax.all_gather(grads, group, axis=0)
    other, gathered = lax.optimization_barrier((other, gathered))
    clips = lax.all_to_all(
        gain_terms + other, "y", split_axis=0, concat_axis=0, tiled=True
    )

    mid_grads = pl.pallas_call(
        norm_body,
        out_shape=jax.ShapeDtypeStruct((512, 512), BF16),
        in_specs=[scalars(), whole(), whole()],
        out_specs=whole(),
        compiler_params=PARAMS,
        name="norm",
    )(place, gathered, edges)
    partial = pl.pallas_call(
        low_kernel_body,
        out_shape=jax.ShapeDtypeStruct((64, 4, 128), F32),
        in_specs=[whole(), whole()],
        out_specs=whole(),
        scratch_shapes=[pltpu.VMEM((8, 144, 512), BF16)],
        compiler_params=PARAMS,
        name="low_conv",
    )(mid_grads, low_all)

    outgoing = pl.pallas_call(
        close_body,
        out_shape=jax.ShapeDtypeStruct((64, 3, 2, 128), BF16),
        in_specs=[whole(), whole()],
        out_specs=whole(),
        compiler_params=PARAMS,
        name="close",
    )(partial, clips)
    outgoing = outgoing.reshape(192, 2, 128)
    incoming = lax.all_to_all(outgoing, shard, split_axis=0, concat_axis=0, tiled=True)

    positions = 8 * 16 * 128 * 8
    grad_in, gain_grad = pl.pallas_call(
        lambda *refs: join_body(1.0 / math.sqrt(positions), *refs),
        out_shape=(
            jax.ShapeDtypeStruct((64, 256), BF16),
            jax.ShapeDtypeStruct((4, 128), F32),
        ),
        in_specs=[whole()],
        out_specs=(whole(), whole()),
        scratch_shapes=[pltpu.VMEM((64, 8, 128), F32)],
        compiler_params=PARAMS,
        name="join",
    )(incoming.reshape(64, 3, 2, 128))
    return (grad_in.reshape(1, 1, 64, 1, 256), gain_grad.reshape(512))


def solution(mesh):
    fine = Mesh(mesh.devices.reshape(2, 4, 4, 8, 2), ("zh", "y", "x", "zl", "c"))
    dp, shard = ("zh", "y"), ("x", "zl", "c")
    return jax.shard_map(
        shards,
        mesh=fine,
        in_specs=(
            P(dp, None, shard, None, None),
            P(dp, None, shard, None, None),
            P(),
            P(shard, None, None),
            P(shard, None, None),
        ),
        out_specs=(P(dp, shard, None, None, None), P()),
        check_vma=False,
    )
```
